256 devices in a mesh: gz: 128 (over y, x_lo, z, core), ta: 2 (over x_hi).
Axes of the slice: x: 4 (x_hi: 2, x_lo: 2; x = x_hi * 2 + x_lo), y: 4, z: 8, core: 2. Of those that a mesh axis runs over, the one named last changes fastest.
Arguments:
- field: bfloat16 [8, 128, 20, 128, 128], P('ta', 'gz'), may hold values from -6 to 6
- cotangent: bfloat16 [8, 128, 20, 128, 128], P('ta', 'gz'), may hold values from -6 to 6
- mix_weight: bfloat16 [20, 20], replicated, may hold values from -1.25 to 1.25
- bias: float32 [20], replicated, may hold values from -0.8 to 0.8
- spectral_weight: float32 [8, 16, 256, 20, 20], P('ta', None, 'gz'), may hold values from -6 to 6
Outputs:
- field_grad: bfloat16 [8, 128, 20, 128, 128], P('ta', 'gz')
- weight_grad: float32 [20, 20], replicated
- bias_grad: float32 [20], replicated
- spectral_grad: float32 [8, 16, 256, 20, 20], P('ta', None, 'gz')
The draws below stay inside these ranges and needn't reach their ends.
All inputs are finite; a program needn't handle non-finite values.
Results may differ from the reference program's by a relative error of at most 0.012.
Values sent between devices are 32-bit elements; how exact they have to be, the bound alone decides.
A program may use at most 64 MiB of HBM per device.

```python
import math
import jax
import jax.numpy as jnp
from jax import lax

C = 20
NX = 128
NY = 128
NT = 8
MX = 16
MY = 16
MZ = 16
MT = 8
NZ = 128


def block_levels(key, dims, split, low, largest):
    loudness, own = 1.0, jax.random.fold_in(key, 6)
    for dim, parts in split:
        heights = jnp.exp(jax.random.uniform(jax.random.fold_in(own, dim), (parts,), jnp.float32, low / len(split), largest / len(split)))
        loudness = loudness * jnp.repeat(heights, dims[dim] // parts).reshape([-1 if axis == dim else 1 for axis in range(len(dims))])
    return loudness


def normal_values(rng, dims, width, bound, split=(), kind=jnp.bfloat16):
    values = width * jax.random.normal(rng, dims, jnp.float32)
    if split:
        values = values * block_levels(rng, dims, split, -0.22, 0.18)
    return jnp.clip(values, -bound, bound).astype(kind)


def setup_inputs(seed: int = 0) -> dict:
    arg_keys = jax.random.split(jax.random.key(seed), 6)
    return {
        "field": normal_values(arg_keys[0], (NT, NZ, C, NX, NY), 1.0, 6.0, ((0, 2), (1, 128))),
        "cotangent": normal_values(arg_keys[1], (NT, NZ, C, NX, NY), 1.0, 6.0, ((0, 2), (1, 128))),
        "mix_weight": normal_values(arg_keys[2], (C, C), C ** -0.5, 1.25),
        "bias": jnp.clip(jax.random.uniform(arg_keys[3], (C,), jnp.float32, -0.8, 0.8), -0.8, 0.8),
        "spectral_weight": normal_values(arg_keys[4], (MT, MZ, MX * MY, C, C), 1.0, 6.0, ((0, 2), (2, 128)), jnp.float32),
    }


def fourier_rows(length, kept):
    half_kept = kept // 2
    frequency = jnp.concatenate([jnp.arange(half_kept + 1, dtype=jnp.int32), jnp.arange(1, kept - half_kept, dtype=jnp.int32)])
    position = jnp.arange(length, dtype=jnp.int32)
    phases = frequency[:, None] * position[None, :] % length
    angles = phases.astype(jnp.float32) * (2.0 * math.pi / length)
    waves = jnp.concatenate([jnp.cos(angles[:half_kept + 1]), jnp.sin(angles[half_kept + 1:])], axis=0)
    return waves * math.sqrt(2.0 / length)

def gelu_slope(values):
    return 0.5 * (1.0 + jax.scipy.special.erf(values * 0.7071067811865476)) + values * jnp.exp(-0.5 * values * values) * 0.3989422804014327

def plane_modes(slab, y_table_bf, x_table):
    y_done = jnp.dot(slab.reshape(-1, NY), y_table_bf.T, preferred_element_type=jnp.float32).reshape(NT, C, NX, MY)
    both = jnp.einsum('tcxb,ax->tcab', y_done, x_table, precision=lax.Precision.HIGHEST)
    return both.reshape(NT, C, MX * MY)

def plane_cells(spectrum, y_table, x_table):
    mode_grid = spectrum.reshape(NT, C, MX, MY)
    partial_y = jnp.einsum('tcab,by->tcay', mode_grid, y_table, precision=lax.Precision.HIGHEST)
    return jnp.einsum('tcay,ax->tcxy', partial_y, x_table, precision=lax.Precision.HIGHEST)

def forward_modes(planes, t_table, z_table):
    in_time = jnp.einsum('ft,ztcm->fzcm', t_table, planes, precision=lax.Precision.HIGHEST)
    return jnp.einsum('ez,fzcm->fecm', z_table, in_time, precision=lax.Precision.HIGHEST)

def back_planes(spectrum, t_table, z_table):
    z_space = jnp.einsum('ez,fecm->fzcm', z_table, spectrum, precision=lax.Precision.HIGHEST)
    return jnp.einsum('ft,fzcm->ztcm', t_table, z_space, precision=lax.Precision.HIGHEST)

def slab_at(array, z_index):
    return lax.dynamic_index_in_dim(array, z_index, 1, keepdims=False)

def reference(field, cotangent, mix_weight, bias, spectral_weight):
    x_table = fourier_rows(NX, MX)
    y_table = fourier_rows(NY, MY)
    z_table = fourier_rows(NZ, MZ)
    t_table = fourier_rows(NT, MT)
    y_table_bf = y_table.astype(jnp.bfloat16)
    z_range = jnp.arange(NZ, dtype=jnp.int32)
    field_planes = lax.map(lambda z_index: plane_modes(slab_at(field, z_index), y_table_bf, x_table), z_range)
    field_spec = forward_modes(field_planes, t_table, z_table)
    mixed_spec = jnp.einsum('femoi,feim->feom', spectral_weight, field_spec, precision=lax.Precision.HIGHEST)
    kernel_planes = back_planes(mixed_spec, t_table, z_table)
    weights_wide = mix_weight.astype(jnp.float32)

    def grad_slab(z_index):
        data = slab_at(field, z_index)
        upstream = slab_at(cotangent, z_index)
        kernel = plane_cells(lax.dynamic_index_in_dim(kernel_planes, z_index, 0, keepdims=False), y_table, x_table)
        linear = jnp.einsum('oi,tixy->toxy', weights_wide, data.astype(jnp.float32), precision=lax.Precision.HIGHEST)
        pre_act = linear + bias[None, :, None, None] + kernel
        grad_pre = (upstream.astype(jnp.float32) * gelu_slope(pre_act)).astype(jnp.bfloat16)
        return (grad_pre, data)

    def first_pass(carry, z_index):
        grad_pre, data = grad_slab(z_index)
        weight_acc = carry[0] + jnp.einsum('toxy,tixy->oi', grad_pre.astype(jnp.float32), data.astype(jnp.float32), precision=lax.Precision.HIGHEST)
        bias_acc = carry[1] + lax.optimization_barrier(jnp.sum(grad_pre.astype(jnp.float32), axis=(0, 2, 3)))
        return ((weight_acc, bias_acc), plane_modes(grad_pre, y_table_bf, x_table))
    start_sums = (jnp.zeros((C, C), jnp.float32), jnp.zeros((C,), jnp.float32))
    sums_out, grad_planes = lax.scan(first_pass, start_sums, z_range)
    grad_spec = forward_modes(grad_planes, t_table, z_table)
    spectral_grad = jnp.einsum('feom,feim->femoi', grad_spec, field_spec, precision=lax.Precision.HIGHEST)
    back_spec = jnp.einsum('femoi,feom->feim', spectral_weight, grad_spec, precision=lax.Precision.HIGHEST)
    back_cells = back_planes(back_spec, t_table, z_table)

    def second_pass(z_index):
        grad_pre, data = grad_slab(z_index)
        bypass = jnp.einsum('oi,toxy->tixy', weights_wide, grad_pre.astype(jnp.float32), precision=lax.Precision.HIGHEST)
        spectral_part = plane_cells(lax.dynamic_index_in_dim(back_cells, z_index, 0, keepdims=False), y_table, x_table)
        return (bypass + spectral_part).astype(jnp.bfloat16)
    field_grad = jnp.moveaxis(lax.map(second_pass, z_range), 0, 1)
    cell_scale = 1.0 / math.sqrt(NX * NY * NZ * NT)
    return (field_grad, sums_out[0] * cell_scale, sums_out[1] * cell_scale, spectral_grad)
```

```python
import math

import jax
import jax.numpy as jnp
import ml_dtypes
import numpy as np
from jax import lax
from jax.experimental import pallas as pl
from jax.experimental.pallas import tpu as pltpu
from jax.sharding import PartitionSpec as P

F32 = jnp.float32
BF16 = jnp.bfloat16
HIGHEST = lax.Precision.HIGHEST
MESH = pl.DeviceIdType.MESH

C = 20
CH = 10
CP = 16
NX = 128
NY = 128
NZ = 128
NT = 8
TD = 4
PLANES = TD * C
GROUPS = 2 * TD


def fourier_rows(length, kept):
    half = kept // 2
    frequency = np.concatenate([np.arange(half + 1), np.arange(1, kept - half)])
    angles = (frequency[:, None] * np.arange(length)[None, :] % length) * (2.0 * math.pi / length)
    waves = np.concatenate([np.cos(angles[: half + 1]), np.sin(angles[half + 1 :])], axis=0)
    return (waves * math.sqrt(2.0 / length)).astype(np.float32)


def two_parts(table):
    high = table.astype(ml_dtypes.bfloat16)
    return high, (table - high.astype(np.float32)).astype(ml_dtypes.bfloat16)


def tables():
    fx, fy = fourier_rows(NX, 16), fourier_rows(NY, 16)
    fz, ft = fourier_rows(NZ, 16), fourier_rows(NT, 8)
    y_fwd = np.zeros((CH, NY, 8, 2, CP), np.float32)
    y_back = np.zeros((8, 2, CP, CH, NY), np.float32)
    for k in range(CH):
        y_fwd[k, :, :, :, k] = fy.T.reshape(NY, 8, 2)
        y_back[:, :, k, k, :] = fy.reshape(8, 2, NY)
    y_fwd = y_fwd.reshape(CH * NY, 256).astype(ml_dtypes.bfloat16)
    yb_high, yb_low = two_parts(y_back.reshape(256, CH * NY))
    fx_high, fx_low = two_parts(fx)
    x_fwd = np.concatenate(
        [np.concatenate([fx_high, fx_high], 1), np.concatenate([fx_low, np.zeros_like(fx_low)], 1)], 0
    )
    x_back = np.concatenate([fx_high.T, fx_high.T, fx_low.T], 1)
    fz_high, fz_low = two_parts(fz)
    z_back = np.concatenate([fz_high.T, fz_high.T, fz_low.T], 1)
    z_fwd = np.repeat(fz, 2, axis=1)
    t_back = np.stack([np.kron(ft[TD * h : TD * h + TD], np.eye(32, dtype=np.float32)) for h in range(2)])
    return {
        "y_fwd": y_fwd, "x_fwd": x_fwd, "z_fwd": z_fwd, "t_fwd": ft, "t_back": t_back,
        "z_back": z_back, "yb_high": yb_high, "yb_low": yb_low, "x_back": x_back,
    }


def gelu_slope(v):
    size = jnp.abs(v)
    bell = jnp.exp(v * v * -0.5)
    d = 1.0 + 0.2316419 * size
    t = pl.reciprocal(d, approx=True)
    t = t * (2.0 - d * t)
    s = 0.3989422804014327
    tail = t * (0.319381530 * s + t * (-0.356563782 * s + t * (1.781477937 * s + t * (-1.821255978 * s + t * (1.330274429 * s)))))
    w = (tail - s * size) * bell
    return jnp.where(v < 0.0, w, 1.0 - w)


def split(values):
    high = values.astype(BF16)
    return high, (values - high.astype(F32)).astype(BF16)


def dot(a, b, precision=None):
    return jnp.dot(a, b, preferred_element_type=F32, precision=precision)


def main_kernel(
    field_h, cot_h, weight_h, mix, bias, t_fwd, x_fwd, z_fwd, z_back, x_back, y_fwd_h, t_back_h, yb_high_h, yb_low_h,
    lin_o, sg_o, cells_o, sums_o,
    field, cot, grad, lin, w_raw, w_t, sg_raw, y_fwd, t_back, yb_high, yb_low, xs, h_rows, mixed_s, mix_kron, acc,
    send1, send2, send3, send4, recv1, recv2, recv3, recv4, ring_s, ring_r, plane_s, plane_r,
    in_sem, w_sem, out_sem, sg_sem, send_sem, recv_sem, small_send, small_recv,
):
    gz, ta = lax.axis_index("gz"), lax.axis_index("ta")
    core = lax.rem(gz, 2)
    z = lax.rem(gz // 2, 8)
    x = ta * 2 + lax.rem(gz // 16, 2)
    y = gz // 32
    me = gz * 2 + ta

    def load(k, src, dst):
        return pltpu.make_async_copy(src, dst, in_sem.at[k])

    field_in = [load(t, field_h.at[pl.ds(t * C, C)], field.at[pl.ds(t * C, C)]) for t in range(TD)]
    rest_in = [
        load(5, cot_h, cot), load(6, t_back_h, t_back), load(7, yb_high_h, yb_high), load(8, yb_low_h, yb_low),
    ]
    table_in = load(4, y_fwd_h, y_fwd)
    w_in = [
        pltpu.make_async_copy(weight_h.at[f, :, b], w_raw.at[pl.ds((f * 2 + b) * 16, 16)], w_sem.at[f * 2 + b])
        for f in range(TD)
        for b in range(2)
    ]
    table_in.start()
    for copy in field_in + w_in + rest_in:
        copy.start()

    barrier = pltpu.get_barrier_semaphore()

    def each_peer(do):
        def step(k, _):
            kz, ky, kx = k // 16, lax.rem(k // 4, 4), lax.rem(k, 4)
            dz = 4 + ((kz + 1) // 2) * (1 - 2 * lax.rem(kz, 2))
            dy = 2 + ((ky + 1) // 2) * (1 - 2 * lax.rem(ky, 2))
            dx = 2 + ((kx + 1) // 2) * (1 - 2 * lax.rem(kx, 2))
            pz, py, px = lax.rem(z + dz, 8), lax.rem(y + dy, 4), lax.rem(x + dx, 4)
            g = py * 32 + lax.rem(px, 2) * 16 + pz * 2
            t = px // 2
            do(g + core, t)
            do(g + 1 - core, t)
            return 0

        lax.fori_loop(0, 127, step, 0)
        do(gz + 1 - 2 * core, ta)

    def greet(g, t):
        pl.semaphore_signal(barrier, inc=1, device_id=(g, t), device_id_type=MESH)

    def exchange(k, source, target):
        pltpu.make_async_copy(source(gz, ta), target, recv_sem.at[k]).start()

        def send(g, t):
            pltpu.make_async_remote_copy(
                src_ref=source(g, t), dst_ref=target, send_sem=send_sem.at[k], recv_sem=recv_sem.at[k],
                device_id=(g, t), device_id_type=MESH,
            ).start()

        each_peer(send)

    def arrived(k, whole):
        pltpu.make_async_copy(whole, whole, recv_sem.at[k]).wait()

    def by_mode(buffer):
        return lambda g, t: buffer.at[g // 8, lax.rem(g, 8) * 2 + t]

    def by_cell(buffer):
        return lambda g, t: buffer.at[g, t]

    def plane_modes(k, planes):
        lhs = jnp.concatenate(planes, axis=1)
        high, low = split(dot(lhs, y_fwd[...]))
        both = dot(x_fwd[...], jnp.concatenate([high, low], axis=0))
        xs[k] = both[:16] + both[16:]

    def mode_messages(send):
        parts = [xs[k] for k in range(GROUPS)]
        for h in range(2):
            mixed = []
            for f in range(TD):
                c = [t_fwd[h * TD + f, ta * TD + t] for t in range(TD)]
                for half in range(2):
                    mixed.append(sum(c[t] * parts[t * 2 + half] for t in range(TD)))
            for r in range(8):
                for j in range(2):
                    send[:, r * 2 + h, j, :] = jnp.concatenate(
                        [mixed[4 * j + i][:, r * 32 : r * 32 + 32] for i in range(4)], axis=1
                    )

    def spectrum(recv):
        flat = [jnp.transpose(dot(z_fwd[...], recv[:, j, :], HIGHEST)) for j in range(2)]
        blocks = []
        for f in range(TD):
            for b in range(2):
                rows = [((f % 2) * 4 + half * 2 + b) * 16 for half in range(2)]
                blocks.append(jnp.concatenate([flat[f // 2][r : r + 16] for r in rows], axis=0))
        return jnp.concatenate(blocks, axis=1)

    def cell_messages(modes, send):
        steps = jnp.transpose(dot(modes, t_back[ta], HIGHEST))
        pieces = []
        for t in range(NT):
            for half in range(2):
                for b in range(2):
                    row = (t * 2 + b) * 16
                    pieces.append(steps[row : row + 16, half * CP : half * CP + CP])
        high, low = split(jnp.concatenate(pieces, axis=1))
        cells = dot(z_back[...], jnp.concatenate([high, low, high], axis=0))
        for k in range(4):
            send[:, k // 2, k % 2, :] = cells[:, k * 128 : k * 128 + 128]

    def cell_rows(recv, out):
        rows = [[recv[:, 2 * r, j, :] + recv[:, 2 * r + 1, j, :] for j in range(2)] for r in range(8)]
        groups = []
        for k in range(GROUPS):
            at = (k % 4) * 32
            groups.append(jnp.concatenate([rows[r][k // 4][:, at : at + 32] for r in range(8)], axis=1))
        high, low = split(jnp.concatenate(groups, axis=0))
        both = jnp.concatenate([high, low], axis=0)
        for n in range(5):
            cut = slice(n * 256, n * 256 + 256)
            wide = dot(both, yb_high[:, cut])
            values = wide[:128] + wide[128:] + dot(high, yb_low[:, cut])
            top, rest = split(values)
            for k in range(GROUPS):
                out[k, 0:16, cut] = top[k * 16 : k * 16 + 16]
                out[k, 16:32, cut] = rest[k * 16 : k * 16 + 16]
                out[k, 32:48, cut] = top[k * 16 : k * 16 + 16]

    def tile_rows(source, t, xt):
        at = pl.multiple_of(xt * 16, 16)
        return source[pl.ds(t * C, C), pl.ds(at, 16), :].reshape(C * 16, NY)

    def pair_rows(source, pair, xt):
        return jnp.concatenate([tile_rows(source, pair * 2, xt), tile_rows(source, pair * 2 + 1, xt)], axis=1)

    def make_kron(transposed):
        pick = (lax.broadcasted_iota(jnp.int32, (C * 16, C), 0) // 16 == lax.broadcasted_iota(jnp.int32, (C * 16, C), 1)).astype(BF16)
        dims = (((1,), (1 if transposed else 0,)), ((), ()))
        tall = lax.dot_general(pick, mix[...], dims, preferred_element_type=F32).astype(BF16)
        wide = lax.dot_general(tall, pick, (((1,), (1,)), ((), ())), preferred_element_type=F32)
        same = lax.rem(lax.broadcasted_iota(jnp.int32, wide.shape, 0), 16) == lax.rem(lax.broadcasted_iota(jnp.int32, wide.shape, 1), 16)
        mix_kron[...] = jnp.where(same, wide, 0.0).astype(BF16)

    def channel_mix(source, add_bias):
        def step(k, _):
            pair, xt = lax.rem(k, 2), k // 2
            out = dot(mix_kron[...], pair_rows(source, pair, xt))
            at = pl.multiple_of(xt * 16, 16)
            for i in range(2):
                for o in range(C):
                    part = out[o * 16 : o * 16 + 16, i * 128 : i * 128 + 128]
                    lin[(pair * 2 + i) * C + o, pl.ds(at, 16), :] = part + bias[o] if add_bias else part
            return 0

        lax.fori_loop(0, 16, step, 0)

    each_peer(greet)
    table_in.wait()
    for t in range(TD):
        field_in[t].wait()

    def field_step(k, _):
        plane_modes(k, [field[k * CH + i] for i in range(CH)])
        return 0

    lax.fori_loop(0, GROUPS, field_step, 0)
    mode_messages(send1)
    pl.semaphore_wait(barrier, 255)
    exchange(0, by_mode(send1), recv1.at[me])
    make_kron(False)
    channel_mix(field, True)
    for copy in w_in + rest_in:
        copy.wait()
    w_t[...] = jnp.zeros_like(w_t)
    for o in range(C):
        turned = jnp.transpose(w_raw[:, o, :])
        w_t[o, 0:CH, :] = turned[:CH]
        w_t[o, CP : CP + CH, :] = turned[CH:]
    mixed_s[...] = jnp.zeros_like(mixed_s)
    arrived(0, recv1)
    field_spec = spectrum(recv1)
    for o in range(C):
        row = o if o < CH else o - CH + CP
        mixed_s[row : row + 1, :] = jnp.sum(w_t[o] * field_spec, axis=0, keepdims=True)
    cell_messages(mixed_s[...], send2)
    exchange(1, by_cell(send2), recv2.at[gz // 8, lax.rem(gz, 8) * 2 + ta])
    make_kron(True)
    acc[...] = jnp.zeros_like(acc)
    arrived(1, recv2)
    cell_rows(recv2, h_rows)

    def grad_step(k, _):
        planes = []
        for n in range(5):
            pair = dot(x_back[...], h_rows[k, :, n * 256 : n * 256 + 256])
            for i in range(2):
                p = k * CH + n * 2 + i
                slope = gelu_slope(lin[p] + pair[:, i * 128 : i * 128 + 128])
                value = (cot[p].astype(F32) * slope).astype(BF16)
                grad[p] = value
                planes.append(value)
        plane_modes(k, planes)
        return 0

    lax.fori_loop(0, GROUPS, grad_step, 0)
    mode_messages(send3)
    exchange(2, by_mode(send3), recv3.at[me])

    def sum_step(k, _):
        pair, xt = lax.rem(k, 2), k // 2
        left = jnp.concatenate([pair_rows(field, pair, xt), jnp.ones((16, 256), BF16)], axis=0)
        acc[...] += lax.dot_general(
            left, pair_rows(grad, pair, xt), (((1,), (1,)), ((), ())), preferred_element_type=F32
        )
        return 0

    lax.fori_loop(0, 16, sum_step, 0)
    shape = acc.shape
    same = lax.rem(lax.broadcasted_iota(jnp.int32, shape, 0), 16) == lax.rem(lax.broadcasted_iota(jnp.int32, shape, 1), 16)
    kept = jnp.where(same, acc[...], 0.0)
    rows = (lax.broadcasted_iota(jnp.int32, (24, shape[0]), 1) // 16 == lax.broadcasted_iota(jnp.int32, (24, shape[0]), 0)).astype(F32)
    lanes = (lax.broadcasted_iota(jnp.int32, (shape[1], 32), 0) // 16 == lax.broadcasted_iota(jnp.int32, (shape[1], 32), 1)).astype(F32)
    sums = dot(dot(rows, kept, HIGHEST), lanes, HIGHEST)
    ring_s[...] = jnp.concatenate([sums[0:8], sums[8:16], sums[16:24], jnp.zeros((8, 32), F32)], axis=1)
    p, q = gz // 16, lax.rem(gz, 16)

    def small(k, source, target, peer):
        return pltpu.make_async_remote_copy(
            src_ref=source, dst_ref=target, send_sem=small_send.at[k], recv_sem=small_recv.at[k],
            device_id=peer, device_id_type=MESH,
        )

    pltpu.make_async_copy(ring_s, ring_r.at[q], small_recv.at[0]).start()

    def ring_step(d, _):
        small(0, ring_s, ring_r.at[q], (p * 16 + lax.rem(q + d, 16), ta)).start()
        return 0

    lax.fori_loop(1, 16, ring_step, 0)
    channel_mix(grad, False)
    lin_out = pltpu.make_async_copy(lin, lin_o, out_sem.at[0])
    lin_out.start()
    arrived(2, recv3)
    grad_spec = spectrum(recv3)
    back = jnp.zeros((32, 128), F32)
    for o in range(C):
        row = o if o < CH else o - CH + CP
        back = back + w_t[o] * grad_spec[row : row + 1]
    cell_messages(back, send4)
    exchange(3, by_cell(send4), recv4.at[gz // 8, lax.rem(gz, 8) * 2 + ta])
    pltpu.make_async_copy(ring_r, ring_r, small_recv.at[0]).wait()
    total = ring_r[0]
    for i in range(1, 16):
        total = total + ring_r[i]
    plane_s[...] = total
    v = p * 2 + ta
    pltpu.make_async_copy(plane_s, plane_r.at[v], small_recv.at[1]).start()

    def plane_step(d, _):
        u = lax.rem(v + d, 16)
        small(1, plane_s, plane_r.at[v], ((u // 2) * 16 + q, lax.rem(u, 2))).start()
        return 0

    lax.fori_loop(1, 16, plane_step, 0)
    for o in range(C):
        row = o if o < CH else o - CH + CP
        turned = jnp.transpose(field_spec * grad_spec[row : row + 1])
        sg_raw[:, o, :] = jnp.concatenate([turned[:, :CH], turned[:, CP : CP + CH]], axis=1)
    sg_out = [
        pltpu.make_async_copy(sg_raw.at[pl.ds((f * 2 + b) * 16, 16)], sg_o.at[f, :, b], sg_sem.at[f * 2 + b])
        for f in range(TD)
        for b in range(2)
    ]
    for copy in sg_out:
        copy.start()
    arrived(3, recv4)
    cell_rows(recv4, cells_o)
    pltpu.make_async_copy(plane_r, plane_r, small_recv.at[1]).wait()
    total = plane_r[0]
    for i in range(1, 16):
        total = total + plane_r[i]
    sums_o[...] = total
    for copy in sg_out:
        copy.wait()
    lin_out.wait()
    for k in range(4):
        sent = recv1.at[pl.ds(0, 255)]
        pltpu.make_async_copy(sent, sent, send_sem.at[k]).wait()
    for k in range(2):
        sent = ring_r.at[pl.ds(0, 15)]
        pltpu.make_async_copy(sent, sent, small_send.at[k]).wait()


def last_kernel(lin, cells, x_back, sums, sg_in, out, wg, bg, sg_out, sem):
    k = pl.program_id(0)
    copy = pltpu.make_async_copy(sg_in, sg_out, sem)

    @pl.when(k == 0)
    def _():
        copy.start()
        scale = 1.0 / math.sqrt(NX * NY * NZ * NT)
        rows = jnp.concatenate([sums[:, 32 * i : 32 * i + 32] for i in range(3)], axis=0) * scale
        wg[...] = jnp.transpose(rows)[:C, :C]
        bg[...] = rows[C : C + 1, :C]

    for n in range(5):
        pair = dot(x_back[...], cells[0, :, n * 256 : n * 256 + 256])
        for i in range(2):
            out[n * 2 + i] = (lin[n * 2 + i] + pair[:, i * 128 : i * 128 + 128]).astype(BF16)

    @pl.when(k == pl.num_programs(0) - 1)
    def _():
        copy.wait()


def per_device(field, cotangent, mix_weight, bias, spectral_weight):
    tab = tables()
    shape = field.shape
    planes = (PLANES, NX, NY)
    any_, vmem, smem = (pl.BlockSpec(memory_space=m) for m in (pl.ANY, pltpu.VMEM, pltpu.SMEM))
    dma = pltpu.SemaphoreType.DMA
    sent, cells = pltpu.VMEM((16, 16, 2, 128), F32), pltpu.VMEM((128, 2, 2, 128), F32)
    rows = pltpu.VMEM((256, 2, 128), F32)
    small = pltpu.VMEM((16, 8, 128), F32)
    lin, sg, h_rows, sums = pl.pallas_call(
        main_kernel,
        out_shape=(
            jax.ShapeDtypeStruct(planes, F32),
            jax.ShapeDtypeStruct(spectral_weight.shape, F32),
            jax.ShapeDtypeStruct((GROUPS, 48, CH * NY), BF16),
            jax.ShapeDtypeStruct((8, 128), F32),
        ),
        in_specs=[any_, any_, any_, vmem, smem, smem, vmem, vmem, vmem, vmem, any_, any_, any_, any_],
        out_specs=(any_, any_, vmem, vmem),
        scratch_shapes=[
            pltpu.VMEM(planes, BF16), pltpu.VMEM(planes, BF16), pltpu.VMEM(planes, BF16), pltpu.VMEM(planes, F32),
            pltpu.VMEM((128, C, C), F32), pltpu.VMEM((C, 32, 128), F32), pltpu.VMEM((128, C, C), F32),
            pltpu.VMEM((CH * NY, 256), BF16), pltpu.VMEM((2, 128, 256), F32),
            pltpu.VMEM((256, CH * NY), BF16), pltpu.VMEM((256, CH * NY), BF16),
            pltpu.VMEM((GROUPS, 16, 256), F32), pltpu.VMEM((GROUPS, 48, CH * NY), BF16), pltpu.VMEM((32, 128), F32),
            pltpu.VMEM((C * 16, C * 16), BF16), pltpu.VMEM((C * 16 + 16, C * 16), F32),
            sent, cells, sent, cells, rows, sent, rows, sent,
            pltpu.VMEM((8, 128), F32), small, pltpu.VMEM((8, 128), F32), small,
            dma((9,)), dma((8,)), dma((1,)), dma((8,)), dma((4,)), dma((4,)), dma((2,)), dma((2,)),
        ],
        compiler_params=pltpu.CompilerParams(collective_id=0, has_side_effects=True, vmem_limit_bytes=56 * 2**20),
    )(
        field.reshape(planes), cotangent.reshape(planes), spectral_weight, mix_weight, bias,
        tab["t_fwd"], tab["x_fwd"], tab["z_fwd"], tab["z_back"], tab["x_back"],
        tab["y_fwd"], tab["t_back"], tab["yb_high"], tab["yb_low"],
    )
    whole = lambda *dims: pl.BlockSpec(dims, lambda k: (0,) * len(dims))
    field_grad, wg, bg, sg = pl.pallas_call(
        last_kernel,
        grid=(GROUPS,),
        out_shape=(
            jax.ShapeDtypeStruct(planes, BF16),
            jax.ShapeDtypeStruct((C, C), F32),
            jax.ShapeDtypeStruct((1, C), F32),
            jax.ShapeDtypeStruct(spectral_weight.shape, F32),
        ),
        in_specs=[
            pl.BlockSpec((CH, NX, NY), lambda k: (k, 0, 0)),
            pl.BlockSpec((1, 48, CH * NY), lambda k: (k, 0, 0)),
            whole(NX, 48), whole(8, 128), any_,
        ],
        out_specs=(pl.BlockSpec((CH, NX, NY), lambda k: (k, 0, 0)), whole(C, C), whole(1, C), any_),
        scratch_shapes=[dma(())],
        compiler_params=pltpu.CompilerParams(vmem_limit_bytes=32 * 2**20),
    )(lin, h_rows, tab["x_back"], sums, sg)
    return field_grad.reshape(shape), wg, bg.reshape(C), sg


def solution(mesh):
    return jax.shard_map(
        per_device,
        mesh=mesh,
        in_specs=(
            P("ta", "gz", None, None, None),
            P("ta", "gz", None, None, None),
            P(),
            P(),
            P("ta", None, "gz", None, None),
        ),
        out_specs=(P("ta", "gz", None, None, None), P(), P(), P("ta", None, "gz", None, None)),
        check_vma=False,
    )
```

```python
import math

import jax
import jax.numpy as jnp
import ml_dtypes
import numpy as np
from jax import lax
from jax.experimental import pallas as pl
from jax.experimental.pallas import tpu as pltpu
from jax.sharding import PartitionSpec as P

F32 = jnp.float32
BF16 = jnp.bfloat16
HIGHEST = lax.Precision.HIGHEST
MESH = pl.DeviceIdType.MESH

C = 20
CH = 10
CP = 16
NX = 128
NY = 128
NZ = 128
NT = 8
TD = 4
PLANES = TD * C
GROUPS = 2 * TD


def fourier_rows(length, kept):
    half = kept // 2
    frequency = np.concatenate([np.arange(half + 1), np.arange(1, kept - half)])
    angles = (frequency[:, None] * np.arange(length)[None, :] % length) * (2.0 * math.pi / length)
    waves = np.concatenate([np.cos(angles[: half + 1]), np.sin(angles[half + 1 :])], axis=0)
    return (waves * math.sqrt(2.0 / length)).astype(np.float32)


def two_parts(table):
    high = table.astype(ml_dtypes.bfloat16)
    return high, (table - high.astype(np.float32)).astype(ml_dtypes.bfloat16)


def tables():
    fx, fy = fourier_rows(NX, 16), fourier_rows(NY, 16)
    fz, ft = fourier_rows(NZ, 16), fourier_rows(NT, 8)
    y_fwd = np.zeros((CH, NY, 8, 2, CP), np.float32)
    y_back = np.zeros((8, 2, CP, CH, NY), np.float32)
    for k in range(CH):
        y_fwd[k, :, :, :, k] = fy.T.reshape(NY, 8, 2)
        y_back[:, :, k, k, :] = fy.reshape(8, 2, NY)
    y_fwd = y_fwd.reshape(CH * NY, 256).astype(ml_dtypes.bfloat16)
    yb_high, yb_low = two_parts(y_back.reshape(256, CH * NY))
    fx_high, fx_low = two_parts(fx)
    x_fwd = np.concatenate(
        [np.concatenate([fx_high, fx_high], 1), np.concatenate([fx_low, np.zeros_like(fx_low)], 1)], 0
    )
    x_back = np.concatenate([fx_high.T, fx_high.T, fx_low.T], 1)
    fz_high, fz_low = two_parts(fz)
    z_back = np.concatenate([fz_high.T, fz_high.T, fz_low.T], 1)
    z_fwd = np.repeat(fz, 2, axis=1)
    t_back = np.einsum("hft,bB,eE->hbfetBE", ft.reshape(2, TD, NT), np.eye(2), np.eye(16))
    t_back = t_back.reshape(2, 128, 256).astype(np.float32)
    return {
        "y_fwd": y_fwd, "x_fwd": x_fwd, "z_fwd": z_fwd, "t_fwd": ft, "t_back": t_back,
        "z_back": z_back, "yb_high": yb_high, "yb_low": yb_low, "x_back": x_back,
    }


def gelu_slope(v):
    size = jnp.abs(v)
    bell = jnp.exp(v * v * -0.5)
    d = 1.0 + 0.2316419 * size
    t = pl.reciprocal(d, approx=True)
    t = t * (2.0 - d * t)
    s = 0.3989422804014327
    tail = t * (0.319381530 * s + t * (-0.356563782 * s + t * (1.781477937 * s + t * (-1.821255978 * s + t * (1.330274429 * s)))))
    w = (tail - s * size) * bell
    return jnp.where(v < 0.0, w, 1.0 - w)


def split(values):
    high = values.astype(BF16)
    return high, (values - high.astype(F32)).astype(BF16)


def dot(a, b, precision=None):
    return jnp.dot(a, b, preferred_element_type=F32, precision=precision)


def main_kernel(
    field_h, cot_h, weight_h, mix_h, bias, t_fwd, x_fwd_h, z_fwd_h, z_back_h, x_back_h, y_fwd_h, t_back_h, yb_high_h, yb_low_h,
    lin_o, sg_o, cells_o, sums_o,
    field, cot, grad, lin, w_raw, w_t, sg_raw, mix, x_fwd, z_fwd, z_back, x_back, y_fwd, t_back, yb_high, yb_low, xs, h_rows, mixed_s, mix_kron, acc,
    send1, send2, send3, send4, recv1, recv2, recv3, recv4, ring_s, ring_r, plane_s, plane_r,
    in_sem, w_sem, out_sem, sg_sem, send_sem, recv_sem, small_send, small_recv,
):
    gz, ta = lax.axis_index("gz"), lax.axis_index("ta")
    core = lax.rem(gz, 2)
    z = lax.rem(gz // 2, 8)
    x = ta * 2 + lax.rem(gz // 16, 2)
    y = gz // 32
    me = gz * 2 + ta

    def load(k, src, dst):
        return pltpu.make_async_copy(src, dst, in_sem.at[k])

    field_in = [load(t, field_h.at[pl.ds(t * C, C)], field.at[pl.ds(t * C, C)]) for t in range(TD)]
    rest_in = [
        load(5, cot_h, cot), load(6, t_back_h, t_back), load(7, yb_high_h, yb_high), load(8, yb_low_h, yb_low),
        load(10, mix_h, mix), load(11, z_fwd_h, z_fwd), load(12, z_back_h, z_back), load(13, x_back_h, x_back),
    ]
    table_in = [load(4, y_fwd_h, y_fwd), load(9, x_fwd_h, x_fwd)]
    w_in = [pltpu.make_async_copy(weight_h, w_raw, w_sem.at[0])]
    for copy in table_in + field_in + w_in + rest_in:
        copy.start()

    barrier = pltpu.get_barrier_semaphore()

    steps = sorted(((dy, dx) for dy in range(4) for dx in range(4)), key=lambda d: -(min(d[0], 4 - d[0]) + min(d[1], 4 - d[1])))
    ys, xs_ = [lax.rem(y + d, 4) for d in range(4)], [lax.rem(x + d, 4) for d in range(4)]
    plane = [(ys[dy] * 2 + lax.rem(xs_[dx], 2), xs_[dx] // 2) for dy, dx in steps]

    def each_peer(do):
        def step(kz, _):
            pz = lax.rem(z + 4 + ((kz + 1) // 2) * (1 - 2 * lax.rem(kz, 2)), 8)
            for p, t in plane:
                do(p, pz, core, t)
                do(p, pz, 1 - core, t)
            return 0

        lax.fori_loop(0, 7, step, 0)
        for p, t in plane[:-1]:
            do(p, z, core, t)
            do(p, z, 1 - core, t)
        do(*plane[-1][:1], z, 1 - core, ta)

    def greet(p, pz, c, t):
        pl.semaphore_signal(barrier, inc=1, device_id=(p * 16 + pz * 2 + c, t), device_id_type=MESH)

    def exchange(k, source, target):
        pltpu.make_async_copy(source(gz // 16, z, core, ta), target, recv_sem.at[k]).start()

        def send(p, pz, c, t):
            pltpu.make_async_remote_copy(
                src_ref=source(p, pz, c, t), dst_ref=target, send_sem=send_sem.at[k], recv_sem=recv_sem.at[k],
                device_id=(p * 16 + pz * 2 + c, t), device_id_type=MESH,
            ).start()

        each_peer(send)

    def arrived(k, whole):
        pltpu.make_async_copy(whole, whole, recv_sem.at[k]).wait()

    def by_mode(buffer):
        return lambda p, pz, c, t: buffer.at[p * 2 + pz // 4, lax.rem(pz, 4) * 4 + c * 2 + t]

    def by_cell(buffer):
        return lambda p, pz, c, t: buffer.at[p * 16 + pz * 2 + c, t]

    def plane_modes(k, planes):
        lhs = jnp.concatenate(planes, axis=1)
        high, low = split(dot(lhs, y_fwd[...]))
        both = dot(x_fwd[...], jnp.concatenate([high, low], axis=0))
        xs[k] = both[:16] + both[16:]

    def mode_messages(send):
        parts = [xs[k] for k in range(GROUPS)]
        for h in range(2):
            mixed = []
            for f in range(TD):
                c = [t_fwd[h * TD + f, ta * TD + t] for t in range(TD)]
                for half in range(2):
                    mixed.append(sum(c[t] * parts[t * 2 + half] for t in range(TD)))
            for r in range(8):
                for j in range(2):
                    send[:, r * 2 + h, j, :] = jnp.concatenate(
                        [mixed[4 * j + i][:, r * 32 : r * 32 + 32] for i in range(4)], axis=1
                    )

    def spectrum(recv):
        flat = [jnp.transpose(dot(z_fwd[...], recv[:, j, :], HIGHEST)) for j in range(2)]
        blocks = []
        for b in range(2):
            for f in range(TD):
                rows = [((f % 2) * 4 + half * 2 + b) * 16 for half in range(2)]
                blocks.append(jnp.concatenate([flat[f // 2][r : r + 16] for r in rows], axis=0))
        return jnp.concatenate(blocks, axis=1)

    def cell_messages(modes, send):
        steps = jnp.transpose(dot(modes, t_back[ta], HIGHEST))
        pieces = []
        for t in range(NT):
            for half in range(2):
                for b in range(2):
                    row = (t * 2 + b) * 16
                    pieces.append(steps[row : row + 16, half * CP : half * CP + CP])
        high, low = split(jnp.concatenate(pieces, axis=1))
        cells = dot(z_back[...], jnp.concatenate([high, low, high], axis=0))
        for k in range(4):
            send[:, k // 2, k % 2, :] = cells[:, k * 128 : k * 128 + 128]

    def cell_rows(recv, out):
        rows = [[recv[:, 2 * r, j, :] + recv[:, 2 * r + 1, j, :] for j in range(2)] for r in range(8)]
        groups = []
        for k in range(GROUPS):
            at = (k % 4) * 32
            groups.append(jnp.concatenate([rows[r][k // 4][:, at : at + 32] for r in range(8)], axis=1))
        high, low = split(jnp.concatenate(groups, axis=0))
        both = jnp.concatenate([high, low], axis=0)
        for n in range(5):
            cut = slice(n * 256, n * 256 + 256)
            wide = dot(both, yb_high[:, cut])
            values = wide[:128] + wide[128:] + dot(high, yb_low[:, cut])
            top, rest = split(values)
            for k in range(GROUPS):
                out[k, 0:16, cut] = top[k * 16 : k * 16 + 16]
                out[k, 16:32, cut] = rest[k * 16 : k * 16 + 16]
                out[k, 32:48, cut] = top[k * 16 : k * 16 + 16]

    def tile_rows(source, t, xt):
        at = pl.multiple_of(xt * 16, 16)
        return source[pl.ds(t * C, C), pl.ds(at, 16), :].reshape(C * 16, NY)

    def pair_rows(source, pair, xt):
        return jnp.concatenate([tile_rows(source, pair * 2, xt), tile_rows(source, pair * 2 + 1, xt)], axis=1)

    def make_kron(transposed):
        pick = (lax.broadcasted_iota(jnp.int32, (C * 16, C), 0) // 16 == lax.broadcasted_iota(jnp.int32, (C * 16, C), 1)).astype(BF16)
        dims = (((1,), (1 if transposed else 0,)), ((), ()))
        tall = lax.dot_general(pick, mix[...], dims, preferred_element_type=F32).astype(BF16)
        wide = lax.dot_general(tall, pick, (((1,), (1,)), ((), ())), preferred_element_type=F32)
        same = lax.rem(lax.broadcasted_iota(jnp.int32, wide.shape, 0), 16) == lax.rem(lax.broadcasted_iota(jnp.int32, wide.shape, 1), 16)
        mix_kron[...] = jnp.where(same, wide, 0.0).astype(BF16)

    def channel_mix(source, add_bias):
        def step(k, _):
            pair, xt = lax.rem(k, 2), k // 2
            out = dot(mix_kron[...], pair_rows(source, pair, xt))
            at = pl.multiple_of(xt * 16, 16)
            for i in range(2):
                for o in range(C):
                    part = out[o * 16 : o * 16 + 16, i * 128 : i * 128 + 128]
                    lin[(pair * 2 + i) * C + o, pl.ds(at, 16), :] = part + bias[o] if add_bias else part
            return 0

        lax.fori_loop(0, 16, step, 0)

    each_peer(greet)
    for copy in table_in + field_in:
        copy.wait()

    def field_step(k, _):
        plane_modes(k, [field[k * CH + i] for i in range(CH)])
        return 0

    lax.fori_loop(0, GROUPS, field_step, 0)
    mode_messages(send1)
    pl.semaphore_wait(barrier, 255)
    exchange(0, by_mode(send1), recv1.at[me])
    for copy in rest_in + w_in:
        copy.wait()
    make_kron(False)
    channel_mix(field, True)
    w_t[...] = jnp.zeros_like(w_t)
    for o in range(C):
        turned = jnp.transpose(jnp.concatenate([w_raw[:, o, b, :] for b in range(2)], axis=0))
        w_t[o, 0:CH, :] = turned[:CH]
        w_t[o, CP : CP + CH, :] = turned[CH:]
    mixed_s[...] = jnp.zeros_like(mixed_s)
    arrived(0, recv1)
    field_spec = spectrum(recv1)
    for o in range(C):
        row = o if o < CH else o - CH + CP
        mixed_s[row : row + 1, :] = jnp.sum(w_t[o] * field_spec, axis=0, keepdims=True)
    cell_messages(mixed_s[...], send2)
    exchange(1, by_cell(send2), recv2.at[gz // 8, lax.rem(gz, 8) * 2 + ta])
    make_kron(True)
    acc[...] = jnp.zeros_like(acc)
    arrived(1, recv2)
    cell_rows(recv2, h_rows)

    def grad_step(k, _):
        planes = []
        for n in range(5):
            pair = dot(x_back[...], h_rows[k, :, n * 256 : n * 256 + 256])
            for i in range(2):
                p = k * CH + n * 2 + i
                slope = gelu_slope(lin[p] + pair[:, i * 128 : i * 128 + 128])
                value = (cot[p].astype(F32) * slope).astype(BF16)
                grad[p] = value
                planes.append(value)
        plane_modes(k, planes)
        return 0

    lax.fori_loop(0, GROUPS, grad_step, 0)
    mode_messages(send3)
    exchange(2, by_mode(send3), recv3.at[me])

    def sum_step(k, _):
        pair, xt = lax.rem(k, 2), k // 2
        left = jnp.concatenate([pair_rows(field, pair, xt), jnp.ones((16, 256), BF16)], axis=0)
        acc[...] += lax.dot_general(
            left, pair_rows(grad, pair, xt), (((1,), (1,)), ((), ())), preferred_element_type=F32
        )
        return 0

    lax.fori_loop(0, 16, sum_step, 0)
    shape = acc.shape
    same = lax.rem(lax.broadcasted_iota(jnp.int32, shape, 0), 16) == lax.rem(lax.broadcasted_iota(jnp.int32, shape, 1), 16)
    kept = jnp.where(same, acc[...], 0.0)
    rows = (lax.broadcasted_iota(jnp.int32, (24, shape[0]), 1) // 16 == lax.broadcasted_iota(jnp.int32, (24, shape[0]), 0)).astype(F32)
    lanes = (lax.broadcasted_iota(jnp.int32, (shape[1], 32), 0) // 16 == lax.broadcasted_iota(jnp.int32, (shape[1], 32), 1)).astype(F32)
    sums = dot(dot(rows, kept, HIGHEST), lanes, HIGHEST)
    ring_s[...] = jnp.concatenate([sums[0:8], sums[8:16], sums[16:24], jnp.zeros((8, 32), F32)], axis=1)
    p, q = gz // 16, lax.rem(gz, 16)

    def small(k, source, target, peer):
        return pltpu.make_async_remote_copy(
            src_ref=source, dst_ref=target, send_sem=small_send.at[k], recv_sem=small_recv.at[k],
            device_id=peer, device_id_type=MESH,
        )

    pltpu.make_async_copy(ring_s, ring_r.at[q], small_recv.at[0]).start()

    def ring_step(d, _):
        small(0, ring_s, ring_r.at[q], (p * 16 + lax.rem(q + d, 16), ta)).start()
        return 0

    lax.fori_loop(1, 16, ring_step, 0)
    arrived(2, recv3)
    grad_spec = spectrum(recv3)
    back = jnp.zeros((32, 128), F32)
    for o in range(C):
        row = o if o < CH else o - CH + CP
        back = back + w_t[o] * grad_spec[row : row + 1]
    cell_messages(back, send4)
    exchange(3, by_cell(send4), recv4.at[gz // 8, lax.rem(gz, 8) * 2 + ta])
    pltpu.make_async_copy(ring_r, ring_r, small_recv.at[0]).wait()
    total = ring_r[0]
    for i in range(1, 16):
        total = total + ring_r[i]
    plane_s[...] = total
    v = p * 2 + ta
    pltpu.make_async_copy(plane_s, plane_r.at[v], small_recv.at[1]).start()

    def plane_step(d, _):
        u = lax.rem(v + d, 16)
        small(1, plane_s, plane_r.at[v], ((u // 2) * 16 + q, lax.rem(u, 2))).start()
        return 0

    lax.fori_loop(1, 16, plane_step, 0)
    for o in range(C):
        row = o if o < CH else o - CH + CP
        turned = jnp.transpose(field_spec * grad_spec[row : row + 1])
        for b in range(2):
            part = turned[b * 64 : b * 64 + 64]
            sg_raw[:, o, b, :] = jnp.concatenate([part[:, :CH], part[:, CP : CP + CH]], axis=1)
    sg_out = [pltpu.make_async_copy(sg_raw, sg_o, sg_sem.at[0])]
    for copy in sg_out:
        copy.start()
    channel_mix(grad, False)
    lin_out = pltpu.make_async_copy(lin, lin_o, out_sem.at[0])
    lin_out.start()
    arrived(3, recv4)
    cell_rows(recv4, cells_o)
    pltpu.make_async_copy(plane_r, plane_r, small_recv.at[1]).wait()
    total = plane_r[0]
    for i in range(1, 16):
        total = total + plane_r[i]
    sums_o[...] = total
    for copy in sg_out:
        copy.wait()
    lin_out.wait()
    for k in range(4):
        sent = recv1.at[pl.ds(0, 255)]
        pltpu.make_async_copy(sent, sent, send_sem.at[k]).wait()
    for k in range(2):
        sent = ring_r.at[pl.ds(0, 15)]
        pltpu.make_async_copy(sent, sent, small_send.at[k]).wait()


def last_kernel(lin, cells, x_back, sums, sg_in, out, wg, bg, sg_out, staged, sem):
    k = pl.program_id(0)
    copy_in = pltpu.make_async_copy(sg_in, staged, sem.at[0])
    copy_out = pltpu.make_async_copy(staged, sg_out, sem.at[1])

    @pl.when(k == 0)
    def _():
        copy_in.start()
        scale = 1.0 / math.sqrt(NX * NY * NZ * NT)
        rows = jnp.concatenate([sums[:, 32 * i : 32 * i + 32] for i in range(3)], axis=0) * scale
        wg[...] = jnp.transpose(rows)[:C, :C]
        bg[...] = rows[C : C + 1, :C]

    for half in range(2):
        for n in range(5):
            pair = dot(x_back[...], cells[half, :, n * 256 : n * 256 + 256])
            for i in range(2):
                p = half * CH + n * 2 + i
                out[p] = (lin[p] + pair[:, i * 128 : i * 128 + 128]).astype(BF16)

    @pl.when(k == 1)
    def _():
        copy_in.wait()
        copy_out.start()

    @pl.when(k == pl.num_programs(0) - 1)
    def _():
        copy_out.wait()


def per_device(field, cotangent, mix_weight, bias, spectral_weight):
    tab = tables()
    shape = field.shape
    planes = (PLANES, NX, NY)
    weight = jnp.transpose(spectral_weight, (0, 1, 3, 2, 4)).reshape(64, C, 2, C)
    modes = (64, C, 2, C)
    whole = lambda *dims: pl.BlockSpec(dims, lambda k: (0,) * len(dims))
    any_, hbm, vmem, smem = (pl.BlockSpec(memory_space=m) for m in (pl.ANY, pltpu.HBM, pltpu.VMEM, pltpu.SMEM))
    dma = pltpu.SemaphoreType.DMA
    sent, cells = pltpu.VMEM((16, 16, 2, 128), F32), pltpu.VMEM((128, 2, 2, 128), F32)
    rows = pltpu.VMEM((256, 2, 128), F32)
    small = pltpu.VMEM((16, 8, 128), F32)
    lin, sg, h_rows, sums = pl.pallas_call(
        main_kernel,
        out_shape=(
            jax.ShapeDtypeStruct(planes, F32),
            jax.ShapeDtypeStruct(modes, F32),
            jax.ShapeDtypeStruct((GROUPS, 48, CH * NY), BF16),
            jax.ShapeDtypeStruct((8, 128), F32),
        ),
        in_specs=[hbm] * 4 + [smem] * 2 + [hbm] * 8,
        out_specs=(any_, any_, vmem, vmem),
        scratch_shapes=[
            pltpu.VMEM(planes, BF16), pltpu.VMEM(planes, BF16), pltpu.VMEM(planes, BF16), pltpu.VMEM(planes, F32),
            pltpu.VMEM(modes, F32), pltpu.VMEM((C, 32, 128), F32), pltpu.VMEM(modes, F32),
            pltpu.VMEM((C, C), BF16), pltpu.VMEM((32, 256), BF16), pltpu.VMEM((16, 256), F32),
            pltpu.VMEM((128, 48), BF16), pltpu.VMEM((128, 48), BF16),
            pltpu.VMEM((CH * NY, 256), BF16), pltpu.VMEM((2, 128, 256), F32),
            pltpu.VMEM((256, CH * NY), BF16), pltpu.VMEM((256, CH * NY), BF16),
            pltpu.VMEM((GROUPS, 16, 256), F32), pltpu.VMEM((GROUPS, 48, CH * NY), BF16), pltpu.VMEM((32, 128), F32),
            pltpu.VMEM((C * 16, C * 16), BF16), pltpu.VMEM((C * 16 + 16, C * 16), F32),
            sent, cells, sent, cells, rows, sent, rows, sent,
            pltpu.VMEM((8, 128), F32), small, pltpu.VMEM((8, 128), F32), small,
            dma((14,)), dma((1,)), dma((1,)), dma((1,)), dma((4,)), dma((4,)), dma((2,)), dma((2,)),
        ],
        compiler_params=pltpu.CompilerParams(collective_id=0, has_side_effects=True, vmem_limit_bytes=57 * 2**20),
    )(
        field.reshape(planes), cotangent.reshape(planes), weight, mix_weight, bias,
        tab["t_fwd"], tab["x_fwd"], tab["z_fwd"], tab["z_back"], tab["x_back"],
        tab["y_fwd"], tab["t_back"], tab["yb_high"], tab["yb_low"],
    )
    field_grad, wg, bg, sg = pl.pallas_call(
        last_kernel,
        grid=(TD,),
        out_shape=(
            jax.ShapeDtypeStruct(planes, BF16),
            jax.ShapeDtypeStruct((C, C), F32),
            jax.ShapeDtypeStruct((1, C), F32),
            jax.ShapeDtypeStruct(modes, F32),
        ),
        in_specs=[
            pl.BlockSpec((C, NX, NY), lambda k: (k, 0, 0)),
            pl.BlockSpec((2, 48, CH * NY), lambda k: (k, 0, 0)),
            whole(NX, 48), whole(8, 128), any_,
        ],
        out_specs=(pl.BlockSpec((C, NX, NY), lambda k: (k, 0, 0)), whole(C, C), whole(1, C), any_),
        scratch_shapes=[pltpu.VMEM(modes, F32), dma((2,))],
        compiler_params=pltpu.CompilerParams(vmem_limit_bytes=60 * 2**20),
    )(lin, h_rows, tab["x_back"], sums, sg)
    sg = jnp.transpose(sg.reshape(TD, 16, C, 2, C), (0, 1, 3, 2, 4))
    return field_grad.reshape(shape), wg, bg.reshape(C), sg


def solution(mesh):
    return jax.shard_map(
        per_device,
        mesh=mesh,
        in_specs=(
            P("ta", "gz", None, None, None),
            P("ta", "gz", None, None, None),
            P(),
            P(),
            P("ta", None, "gz", None, None),
        ),
        out_specs=(P("ta", "gz", None, None, None), P(), P(), P("ta", None, "gz", None, None)),
        check_vma=False,
    )
```

```python
import math

import jax
import jax.numpy as jnp
import ml_dtypes
import numpy as np
from jax import lax
from jax.experimental import pallas as pl
from jax.experimental.pallas import tpu as pltpu
from jax.sharding import PartitionSpec as P

F32 = jnp.float32
BF16 = jnp.bfloat16
HIGHEST = lax.Precision.HIGHEST
MESH = pl.DeviceIdType.MESH

C = 20
CH = 10
CP = 16
NX = 128
NY = 128
NZ = 128
NT = 8
TD = 4
PLANES = TD * C
GROUPS = 2 * TD


def fourier_rows(length, kept):
    half = kept // 2
    frequency = np.concatenate([np.arange(half + 1), np.arange(1, kept - half)])
    angles = (frequency[:, None] * np.arange(length)[None, :] % length) * (2.0 * math.pi / length)
    waves = np.concatenate([np.cos(angles[: half + 1]), np.sin(angles[half + 1 :])], axis=0)
    return (waves * math.sqrt(2.0 / length)).astype(np.float32)


def two_parts(table):
    high = table.astype(ml_dtypes.bfloat16)
    return high, (table - high.astype(np.float32)).astype(ml_dtypes.bfloat16)


def tables():
    fx, fy = fourier_rows(NX, 16), fourier_rows(NY, 16)
    fz, ft = fourier_rows(NZ, 16), fourier_rows(NT, 8)
    y_fwd = np.zeros((CH, NY, 8, 2, CP), np.float32)
    y_back = np.zeros((8, 2, CP, CH, NY), np.float32)
    for k in range(CH):
        y_fwd[k, :, :, :, k] = fy.T.reshape(NY, 8, 2)
        y_back[:, :, k, k, :] = fy.reshape(8, 2, NY)
    y_fwd = y_fwd.reshape(CH * NY, 256).astype(ml_dtypes.bfloat16)
    yb_high, yb_low = two_parts(y_back.reshape(256, CH * NY))
    fx_high, fx_low = two_parts(fx)
    x_fwd = np.concatenate(
        [np.concatenate([fx_high, fx_high], 1), np.concatenate([fx_low, np.zeros_like(fx_low)], 1)], 0
    )
    x_back = np.concatenate([fx_high.T, fx_high.T, fx_low.T], 1)
    fz_high, fz_low = two_parts(fz)
    z_back = np.concatenate([fz_high.T, fz_high.T, fz_low.T], 1)
    z_fwd = np.repeat(fz, 2, axis=1)
    t_back = np.einsum("hft,bB,eE->hbfetBE", ft.reshape(2, TD, NT), np.eye(2), np.eye(16))
    t_back = t_back.reshape(2, 128, 256).astype(np.float32)
    return {
        "y_fwd": y_fwd, "x_fwd": x_fwd, "z_fwd": z_fwd, "t_fwd": ft, "t_back": t_back,
        "z_back": z_back, "yb_high": yb_high, "yb_low": yb_low, "x_back": x_back,
    }


def gelu_slope(v):
    size = jnp.abs(v)
    bell = jnp.exp2(v * v * -0.7213475204444817)
    d = 1.0 + 0.2316419 * size
    t = pl.reciprocal(d, approx=True)
    t = t * (2.0 - d * t)
    s = 0.3989422804014327
    tail = t * (0.319381530 * s + t * (-0.356563782 * s + t * (1.781477937 * s + t * (-1.821255978 * s + t * (1.330274429 * s)))))
    w = (tail - s * size) * bell
    return jnp.where(v < 0.0, w, 1.0 - w)


def split(values):
    high = values.astype(BF16)
    return high, (values - high.astype(F32)).astype(BF16)


def dot(a, b, precision=None):
    return jnp.dot(a, b, preferred_element_type=F32, precision=precision)


def main_kernel(
    field_h, cot_h, weight_h, mix_h, bias, t_fwd, x_fwd_h, z_fwd_h, z_back_h, x_back_h, y_fwd_h, t_back_h, yb_high_h, yb_low_h,
    lin_o, sg_o, cells_o, sums_o,
    field, cot, grad, lin, w_raw, w_t, sg_raw, mix, x_fwd, z_fwd, z_back, x_back, y_fwd, t_back, yb_high, yb_low, xs, h_rows, mixed_s, mix_kron, acc,
    send1, send2, send3, send4, recv1, recv2, recv3, recv4, ring_s, ring_r, plane_s, plane_r,
    in_sem, w_sem, out_sem, sg_sem, send_sem, recv_sem, small_send, small_recv,
):
    gz, ta = lax.axis_index("gz"), lax.axis_index("ta")
    core = lax.rem(gz, 2)
    z = lax.rem(gz // 2, 8)
    x = ta * 2 + lax.rem(gz // 16, 2)
    y = gz // 32
    me = gz * 2 + ta

    def load(k, src, dst):
        return pltpu.make_async_copy(src, dst, in_sem.at[k])

    field_in = [load(t, field_h.at[pl.ds(t * C, C)], field.at[pl.ds(t * C, C)]) for t in range(TD)]
    rest_in = [
        load(5, cot_h, cot), load(6, t_back_h, t_back), load(7, yb_high_h, yb_high), load(8, yb_low_h, yb_low),
        load(10, mix_h, mix), load(11, z_fwd_h, z_fwd), load(12, z_back_h, z_back), load(13, x_back_h, x_back),
    ]
    table_in = [load(4, y_fwd_h, y_fwd), load(9, x_fwd_h, x_fwd)]
    w_in = [pltpu.make_async_copy(weight_h, w_raw, w_sem.at[0])]
    barrier = pltpu.get_barrier_semaphore()

    steps = sorted(((dy, dx) for dy in range(4) for dx in range(4)), key=lambda d: -(min(d[0], 4 - d[0]) + min(d[1], 4 - d[1])))
    ys, xs_ = [lax.rem(y + d, 4) for d in range(4)], [lax.rem(x + d, 4) for d in range(4)]
    plane = [(ys[dy] * 2 + lax.rem(xs_[dx], 2), xs_[dx] // 2) for dy, dx in steps]

    def each_peer(do):
        def step(kz, _):
            pz = lax.rem(z + 4 + ((kz + 1) // 2) * (1 - 2 * lax.rem(kz, 2)), 8)
            for p, t in plane:
                do(p, pz, core, t)
                do(p, pz, 1 - core, t)
            return 0

        lax.fori_loop(0, 7, step, 0)
        for p, t in plane[:-1]:
            do(p, z, core, t)
            do(p, z, 1 - core, t)
        do(*plane[-1][:1], z, 1 - core, ta)

    def greet(p, pz, c, t):
        pl.semaphore_signal(barrier, inc=1, device_id=(p * 16 + pz * 2 + c, t), device_id_type=MESH)

    def exchange(k, source, target):
        pltpu.make_async_copy(source(gz // 16, z, core, ta), target, recv_sem.at[k]).start()

        def send(p, pz, c, t):
            pltpu.make_async_remote_copy(
                src_ref=source(p, pz, c, t), dst_ref=target, send_sem=send_sem.at[k], recv_sem=recv_sem.at[k],
                device_id=(p * 16 + pz * 2 + c, t), device_id_type=MESH,
            ).start()

        each_peer(send)

    def arrived(k, whole):
        pltpu.make_async_copy(whole, whole, recv_sem.at[k]).wait()

    def by_mode(buffer):
        return lambda p, pz, c, t: buffer.at[p * 2 + pz // 4, lax.rem(pz, 4) * 4 + c * 2 + t]

    def by_cell(buffer):
        return lambda p, pz, c, t: buffer.at[p * 16 + pz * 2 + c, t]

    def plane_modes(t, source):
        halves = [[source[t * C + half * CH + i] for i in range(CH)] for half in range(2)]
        y_done = dot(jnp.concatenate([jnp.concatenate(h, axis=1) for h in halves], axis=0), y_fwd[...])
        for half in range(2):
            high, low = split(y_done[half * NX : half * NX + NX])
            both = dot(x_fwd[...], jnp.concatenate([high, low], axis=0))
            xs[t * 2 + half] = both[:16] + both[16:]

    def mode_messages(send):
        parts = [xs[k] for k in range(GROUPS)]
        for h in range(2):
            mixed = []
            for f in range(TD):
                c = [t_fwd[h * TD + f, ta * TD + t] for t in range(TD)]
                for half in range(2):
                    mixed.append(sum(c[t] * parts[t * 2 + half] for t in range(TD)))
            for r in range(8):
                for j in range(2):
                    send[:, r * 2 + h, j, :] = jnp.concatenate(
                        [mixed[4 * j + i][:, r * 32 : r * 32 + 32] for i in range(4)], axis=1
                    )

    def spectrum(recv):
        flat = [jnp.transpose(dot(z_fwd[...], recv[:, j, :], HIGHEST)) for j in range(2)]
        blocks = []
        for b in range(2):
            for f in range(TD):
                rows = [((f % 2) * 4 + half * 2 + b) * 16 for half in range(2)]
                blocks.append(jnp.concatenate([flat[f // 2][r : r + 16] for r in rows], axis=0))
        return jnp.concatenate(blocks, axis=1)

    def cell_messages(modes, send):
        steps = jnp.transpose(dot(modes, t_back[ta], HIGHEST))
        pieces = []
        for t in range(NT):
            for half in range(2):
                for b in range(2):
                    row = (t * 2 + b) * 16
                    pieces.append(steps[row : row + 16, half * CP : half * CP + CP])
        high, low = split(jnp.concatenate(pieces, axis=1))
        cells = dot(z_back[...], jnp.concatenate([high, low, high], axis=0))
        for k in range(4):
            send[:, k // 2, k % 2, :] = cells[:, k * 128 : k * 128 + 128]

    def cell_rows(recv, out):
        rows = [[recv[:, 2 * r, j, :] + recv[:, 2 * r + 1, j, :] for j in range(2)] for r in range(8)]
        groups = []
        for k in range(GROUPS):
            at = (k % 4) * 32
            groups.append(jnp.concatenate([rows[r][k // 4][:, at : at + 32] for r in range(8)], axis=1))
        high, low = split(jnp.concatenate(groups, axis=0))
        both = jnp.concatenate([high, low], axis=0)
        for n in range(5):
            cut = slice(n * 256, n * 256 + 256)
            wide = dot(both, yb_high[:, cut])
            values = wide[:128] + wide[128:] + dot(high, yb_low[:, cut])
            top, rest = split(values)
            for k in range(GROUPS):
                out[k, 0:16, cut] = top[k * 16 : k * 16 + 16]
                out[k, 16:32, cut] = rest[k * 16 : k * 16 + 16]
                out[k, 32:48, cut] = top[k * 16 : k * 16 + 16]

    def tile_rows(source, t, xt):
        at = pl.multiple_of(xt * 16, 16)
        return source[pl.ds(t * C, C), pl.ds(at, 16), :].reshape(C * 16, NY)

    def pair_rows(source, pair, xt):
        return jnp.concatenate([tile_rows(source, pair * 2, xt), tile_rows(source, pair * 2 + 1, xt)], axis=1)

    def make_kron(transposed):
        pick = (lax.broadcasted_iota(jnp.int32, (C * 16, C), 0) // 16 == lax.broadcasted_iota(jnp.int32, (C * 16, C), 1)).astype(BF16)
        dims = (((1,), (1 if transposed else 0,)), ((), ()))
        tall = lax.dot_general(pick, mix[...], dims, preferred_element_type=F32).astype(BF16)
        wide = lax.dot_general(tall, pick, (((1,), (1,)), ((), ())), preferred_element_type=F32)
        same = lax.rem(lax.broadcasted_iota(jnp.int32, wide.shape, 0), 16) == lax.rem(lax.broadcasted_iota(jnp.int32, wide.shape, 1), 16)
        mix_kron[...] = jnp.where(same, wide, 0.0).astype(BF16)

    def channel_mix(source, add_bias):
        def step(k, _):
            pair, xt = lax.rem(k, 2), k // 2
            out = dot(mix_kron[...], pair_rows(source, pair, xt))
            at = pl.multiple_of(xt * 16, 16)
            for i in range(2):
                for o in range(C):
                    part = out[o * 16 : o * 16 + 16, i * 128 : i * 128 + 128]
                    lin[(pair * 2 + i) * C + o, pl.ds(at, 16), :] = part + bias[o] if add_bias else part
            return 0

        lax.fori_loop(0, 16, step, 0)

    each_peer(greet)
    for copy in table_in + field_in + w_in + rest_in:
        copy.start()
    for copy in table_in + field_in:
        copy.wait()

    def field_step(k, _):
        plane_modes(k, field)
        return 0

    lax.fori_loop(0, TD, field_step, 0)
    mode_messages(send1)
    pl.semaphore_wait(barrier, 255)
    exchange(0, by_mode(send1), recv1.at[me])
    for copy in rest_in + w_in:
        copy.wait()
    make_kron(False)
    channel_mix(field, True)
    w_t[...] = jnp.zeros_like(w_t)
    for o in range(C):
        turned = jnp.transpose(jnp.concatenate([w_raw[:, o, b, :] for b in range(2)], axis=0))
        w_t[o, 0:CH, :] = turned[:CH]
        w_t[o, CP : CP + CH, :] = turned[CH:]
    mixed_s[...] = jnp.zeros_like(mixed_s)
    arrived(0, recv1)
    field_spec = spectrum(recv1)
    for o in range(C):
        row = o if o < CH else o - CH + CP
        mixed_s[row : row + 1, :] = jnp.sum(w_t[o] * field_spec, axis=0, keepdims=True)
    cell_messages(mixed_s[...], send2)
    exchange(1, by_cell(send2), recv2.at[gz // 8, lax.rem(gz, 8) * 2 + ta])
    make_kron(True)
    acc[...] = jnp.zeros_like(acc)
    arrived(1, recv2)
    cell_rows(recv2, h_rows)

    def grad_step(t, _):
        for half in range(2):
            for n in range(5):
                pair = dot(x_back[...], h_rows[t * 2 + half, :, n * 256 : n * 256 + 256])
                for i in range(2):
                    p = t * C + half * CH + n * 2 + i
                    slope = gelu_slope(lin[p] + pair[:, i * 128 : i * 128 + 128])
                    grad[p] = (cot[p].astype(F32) * slope).astype(BF16)
        plane_modes(t, grad)
        return 0

    lax.fori_loop(0, TD, grad_step, 0, unroll=2)
    mode_messages(send3)
    exchange(2, by_mode(send3), recv3.at[me])

    def sum_step(k, _):
        pair, xt = lax.rem(k, 2), k // 2
        left = jnp.concatenate([pair_rows(field, pair, xt), jnp.ones((16, 256), BF16)], axis=0)
        acc[...] += lax.dot_general(
            left, pair_rows(grad, pair, xt), (((1,), (1,)), ((), ())), preferred_element_type=F32
        )
        return 0

    lax.fori_loop(0, 16, sum_step, 0)
    shape = acc.shape
    same = lax.rem(lax.broadcasted_iota(jnp.int32, shape, 0), 16) == lax.rem(lax.broadcasted_iota(jnp.int32, shape, 1), 16)
    kept = jnp.where(same, acc[...], 0.0)
    rows = (lax.broadcasted_iota(jnp.int32, (24, shape[0]), 1) // 16 == lax.broadcasted_iota(jnp.int32, (24, shape[0]), 0)).astype(F32)
    lanes = (lax.broadcasted_iota(jnp.int32, (shape[1], 32), 0) // 16 == lax.broadcasted_iota(jnp.int32, (shape[1], 32), 1)).astype(F32)
    sums = dot(dot(rows, kept, HIGHEST), lanes, HIGHEST)
    ring_s[...] = jnp.concatenate([sums[0:8], sums[8:16], sums[16:24], jnp.zeros((8, 32), F32)], axis=1)
    p, q = gz // 16, lax.rem(gz, 16)

    def small(k, source, target, peer):
        return pltpu.make_async_remote_copy(
            src_ref=source, dst_ref=target, send_sem=small_send.at[k], recv_sem=small_recv.at[k],
            device_id=peer, device_id_type=MESH,
        )

    pltpu.make_async_copy(ring_s, ring_r.at[q], small_recv.at[0]).start()

    def ring_step(d, _):
        small(0, ring_s, ring_r.at[q], (p * 16 + lax.rem(q + d, 16), ta)).start()
        return 0

    lax.fori_loop(1, 16, ring_step, 0)
    arrived(2, recv3)
    grad_spec = spectrum(recv3)
    back = jnp.zeros((32, 128), F32)
    for o in range(C):
        row = o if o < CH else o - CH + CP
        back = back + w_t[o] * grad_spec[row : row + 1]
    cell_messages(back, send4)
    exchange(3, by_cell(send4), recv4.at[gz // 8, lax.rem(gz, 8) * 2 + ta])
    pltpu.make_async_copy(ring_r, ring_r, small_recv.at[0]).wait()
    total = ring_r[0]
    for i in range(1, 16):
        total = total + ring_r[i]
    plane_s[...] = total
    v = p * 2 + ta
    pltpu.make_async_copy(plane_s, plane_r.at[v], small_recv.at[1]).start()

    def plane_step(d, _):
        u = lax.rem(v + d, 16)
        small(1, plane_s, plane_r.at[v], ((u // 2) * 16 + q, lax.rem(u, 2))).start()
        return 0

    lax.fori_loop(1, 16, plane_step, 0)
    for o in range(C):
        row = o if o < CH else o - CH + CP
        turned = jnp.transpose(field_spec * grad_spec[row : row + 1])
        for b in range(2):
            part = turned[b * 64 : b * 64 + 64]
            sg_raw[:, o, b, :] = jnp.concatenate([part[:, :CH], part[:, CP : CP + CH]], axis=1)
    sg_out = [pltpu.make_async_copy(sg_raw, sg_o, sg_sem.at[0])]
    for copy in sg_out:
        copy.start()
    channel_mix(grad, False)
    lin_out = pltpu.make_async_copy(lin, lin_o, out_sem.at[0])
    lin_out.start()
    arrived(3, recv4)
    cell_rows(recv4, cells_o)
    pltpu.make_async_copy(plane_r, plane_r, small_recv.at[1]).wait()
    total = plane_r[0]
    for i in range(1, 16):
        total = total + plane_r[i]
    sums_o[...] = total
    for copy in sg_out:
        copy.wait()
    lin_out.wait()
    for k in range(4):
        sent = recv1.at[pl.ds(0, 255)]
        pltpu.make_async_copy(sent, sent, send_sem.at[k]).wait()
    for k in range(2):
        sent = ring_r.at[pl.ds(0, 15)]
        pltpu.make_async_copy(sent, sent, small_send.at[k]).wait()


def last_kernel(
    lin_h, cells_h, x_back_h, sums_h, sg_h, out_h, wg_h, bg_h, sg_out_h,
    lin, cells, x_back, sums, staged, out, wg, bg, lin_sem, cells_sem, out_sem, sem,
):
    def part(k, n=1):
        return pl.ds(k * n, n)

    x_in = pltpu.make_async_copy(x_back_h, x_back, sem.at[0])
    sums_in = pltpu.make_async_copy(sums_h, sums, sem.at[1])
    sg_in = pltpu.make_async_copy(sg_h, staged, sem.at[2])
    sg_out = pltpu.make_async_copy(staged, sg_out_h, sem.at[3])
    wg_out = pltpu.make_async_copy(wg, wg_h, sem.at[4])
    bg_out = pltpu.make_async_copy(bg, bg_h, sem.at[5])
    cells_in = [pltpu.make_async_copy(cells_h.at[part(k)], cells.at[part(k)], cells_sem.at[k]) for k in range(GROUPS)]
    lin_in = [pltpu.make_async_copy(lin_h.at[part(k, CH)], lin.at[part(k, CH)], lin_sem.at[k]) for k in range(GROUPS)]
    field_out = [pltpu.make_async_copy(out.at[part(k, CH)], out_h.at[part(k, CH)], out_sem.at[k]) for k in range(GROUPS)]
    x_in.start()
    for k in range(GROUPS):
        cells_in[k].start()
        lin_in[k].start()
        if k == 1:
            sums_in.start()
            sg_in.start()
    x_in.wait()
    for k in range(GROUPS):
        cells_in[k].wait()
        lin_in[k].wait()
        for n in range(5):
            pair = dot(x_back[...], cells[k, :, n * 256 : n * 256 + 256])
            for i in range(2):
                p = k * CH + n * 2 + i
                out[p] = (lin[p] + pair[:, i * 128 : i * 128 + 128]).astype(BF16)
        field_out[k].start()
        if k == 3:
            sums_in.wait()
            scale = 1.0 / math.sqrt(NX * NY * NZ * NT)
            rows = jnp.concatenate([sums[:, 32 * i : 32 * i + 32] for i in range(3)], axis=0) * scale
            wg[...] = jnp.transpose(rows)[:C, :C]
            bg[...] = rows[C : C + 1, :C]
            wg_out.start()
            bg_out.start()
            sg_in.wait()
            sg_out.start()
    for copy in [*field_out, wg_out, bg_out, sg_out]:
        copy.wait()


def per_device(field, cotangent, mix_weight, bias, spectral_weight):
    tab = tables()
    shape = field.shape
    planes = (PLANES, NX, NY)
    weight = jnp.transpose(spectral_weight, (0, 1, 3, 2, 4)).reshape(64, C, 2, C)
    modes = (64, C, 2, C)
    any_, hbm, vmem, smem = (pl.BlockSpec(memory_space=m) for m in (pl.ANY, pltpu.HBM, pltpu.VMEM, pltpu.SMEM))
    dma = pltpu.SemaphoreType.DMA
    sent, cells = pltpu.VMEM((16, 16, 2, 128), F32), pltpu.VMEM((128, 2, 2, 128), F32)
    rows = pltpu.VMEM((256, 2, 128), F32)
    small = pltpu.VMEM((16, 8, 128), F32)
    lin, sg, h_rows, sums = pl.pallas_call(
        main_kernel,
        out_shape=(
            jax.ShapeDtypeStruct(planes, F32),
            jax.ShapeDtypeStruct(modes, F32),
            jax.ShapeDtypeStruct((GROUPS, 48, CH * NY), BF16),
            jax.ShapeDtypeStruct((8, 128), F32),
        ),
        in_specs=[hbm] * 4 + [smem] * 2 + [hbm] * 8,
        out_specs=(any_, any_, vmem, vmem),
        scratch_shapes=[
            pltpu.VMEM(planes, BF16), pltpu.VMEM(planes, BF16), pltpu.VMEM(planes, BF16), pltpu.VMEM(planes, F32),
            pltpu.VMEM(modes, F32), pltpu.VMEM((C, 32, 128), F32), pltpu.VMEM(modes, F32),
            pltpu.VMEM((C, C), BF16), pltpu.VMEM((32, 256), BF16), pltpu.VMEM((16, 256), F32),
            pltpu.VMEM((128, 48), BF16), pltpu.VMEM((128, 48), BF16),
            pltpu.VMEM((CH * NY, 256), BF16), pltpu.VMEM((2, 128, 256), F32),
            pltpu.VMEM((256, CH * NY), BF16), pltpu.VMEM((256, CH * NY), BF16),
            pltpu.VMEM((GROUPS, 16, 256), F32), pltpu.VMEM((GROUPS, 48, CH * NY), BF16), pltpu.VMEM((32, 128), F32),
            pltpu.VMEM((C * 16, C * 16), BF16), pltpu.VMEM((C * 16 + 16, C * 16), F32),
            sent, cells, sent, cells, rows, sent, rows, sent,
            pltpu.VMEM((8, 128), F32), small, pltpu.VMEM((8, 128), F32), small,
            dma((14,)), dma((1,)), dma((1,)), dma((1,)), dma((4,)), dma((4,)), dma((2,)), dma((2,)),
        ],
        compiler_params=pltpu.CompilerParams(collective_id=0, has_side_effects=True, vmem_limit_bytes=57 * 2**20),
    )(
        field.reshape(planes), cotangent.reshape(planes), weight, mix_weight, bias,
        tab["t_fwd"], tab["x_fwd"], tab["z_fwd"], tab["z_back"], tab["x_back"],
        tab["y_fwd"], tab["t_back"], tab["yb_high"], tab["yb_low"],
    )
    field_grad, wg, bg, sg = pl.pallas_call(
        last_kernel,
        out_shape=(
            jax.ShapeDtypeStruct(planes, BF16),
            jax.ShapeDtypeStruct((C, C), F32),
            jax.ShapeDtypeStruct((1, C), F32),
            jax.ShapeDtypeStruct(modes, F32),
        ),
        in_specs=[any_] * 5,
        out_specs=(any_,) * 4,
        scratch_shapes=[
            pltpu.VMEM(planes, F32), pltpu.VMEM((GROUPS, 48, CH * NY), BF16), pltpu.VMEM((NX, 48), BF16),
            pltpu.VMEM((8, 128), F32), pltpu.VMEM(modes, F32), pltpu.VMEM(planes, BF16),
            pltpu.VMEM((C, C), F32), pltpu.VMEM((1, C), F32),
            dma((GROUPS,)), dma((GROUPS,)), dma((GROUPS,)), dma((6,)),
        ],
        compiler_params=pltpu.CompilerParams(vmem_limit_bytes=60 * 2**20),
    )(lin, h_rows, tab["x_back"], sums, sg)
    sg = jnp.transpose(sg.reshape(TD, 16, C, 2, C), (0, 1, 3, 2, 4))
    return field_grad.reshape(shape), wg, bg.reshape(C), sg


def solution(mesh):
    return jax.shard_map(
        per_device,
        mesh=mesh,
        in_specs=(
            P("ta", "gz", None, None, None),
            P("ta", "gz", None, None, None),
            P(),
            P(),
            P("ta", None, "gz", None, None),
        ),
        out_specs=(P("ta", "gz", None, None, None), P(), P(), P("ta", None, "gz", None, None)),
        check_vma=False,
    )
```

```python
import math

import jax
import jax.numpy as jnp
import ml_dtypes
import numpy as np
from jax import lax
from jax.experimental import pallas as pl
from jax.experimental.pallas import tpu as pltpu
from jax.sharding import PartitionSpec as P

F32 = jnp.float32
BF16 = jnp.bfloat16
HIGHEST = lax.Precision.HIGHEST
MESH = pl.DeviceIdType.MESH

C = 20
CH = 10
CP = 16
NX = 128
NY = 128
NZ = 128
NT = 8
TD = 4
PLANES = TD * C
GROUPS = 2 * TD


def fourier_rows(length, kept):
    half = kept // 2
    frequency = np.concatenate([np.arange(half + 1), np.arange(1, kept - half)])
    angles = (frequency[:, None] * np.arange(length)[None, :] % length) * (2.0 * math.pi / length)
    waves = np.concatenate([np.cos(angles[: half + 1]), np.sin(angles[half + 1 :])], axis=0)
    return (waves * math.sqrt(2.0 / length)).astype(np.float32)


def two_parts(table):
    high = table.astype(ml_dtypes.bfloat16)
    return high, (table - high.astype(np.float32)).astype(ml_dtypes.bfloat16)


def tables():
    fx, fy = fourier_rows(NX, 16), fourier_rows(NY, 16)
    fz, ft = fourier_rows(NZ, 16), fourier_rows(NT, 8)
    y_fwd = np.zeros((CH, NY, 8, 2, CP), np.float32)
    y_back = np.zeros((8, 2, CP, CH, NY), np.float32)
    for k in range(CH):
        y_fwd[k, :, :, :, k] = fy.T.reshape(NY, 8, 2)
        y_back[:, :, k, k, :] = fy.reshape(8, 2, NY)
    y_fwd = y_fwd.reshape(CH * NY, 256).astype(ml_dtypes.bfloat16)
    yb_high, yb_low = two_parts(y_back.reshape(256, CH * NY))
    fx_high, fx_low = two_parts(fx)
    x_fwd = np.concatenate(
        [np.concatenate([fx_high, fx_high], 1), np.concatenate([fx_low, np.zeros_like(fx_low)], 1)], 0
    )
    x_back = np.concatenate([fx_high.T, fx_high.T, fx_low.T], 1)
    fz_high, fz_low = two_parts(fz)
    z_back = np.concatenate([fz_high.T, fz_high.T, fz_low.T], 1)
    z_fwd = np.repeat(fz, 2, axis=1)
    t_back = np.einsum("hft,bB,eE->hbfetBE", ft.reshape(2, TD, NT), np.eye(2), np.eye(16))
    t_back = t_back.reshape(2, 128, 256).astype(np.float32)
    return {
        "y_fwd": y_fwd, "x_fwd": x_fwd, "z_fwd": z_fwd, "t_fwd": ft, "t_back": t_back,
        "z_back": z_back, "yb_high": yb_high, "yb_low": yb_low, "x_back": x_back,
    }


def gelu_slope(v):
    size = jnp.abs(v)
    bell = jnp.exp2(v * v * -0.7213475204444817)
    d = 1.0 + 0.2316419 * size
    t = pl.reciprocal(d, approx=True)
    t = t * (2.0 - d * t)
    s = 0.3989422804014327
    tail = t * (0.319381530 * s + t * (-0.356563782 * s + t * (1.781477937 * s + t * (-1.821255978 * s + t * (1.330274429 * s)))))
    w = (tail - s * size) * bell
    return jnp.where(v < 0.0, w, 1.0 - w)


def split(values):
    high = values.astype(BF16)
    return high, (values - high.astype(F32)).astype(BF16)


def dot(a, b, precision=None):
    return jnp.dot(a, b, preferred_element_type=F32, precision=precision)


def main_kernel(
    field_h, cot_h, weight_h, mix_h, bias, t_fwd, x_fwd_h, z_fwd_h, z_back_h, x_back_h, y_fwd_h, t_back_h, yb_high_h, yb_low_h,
    lin_o, sg_o, cells_o, sums_o,
    field, cot, grad, lin, w_raw, w_t, sg_raw, mix, x_fwd, z_fwd, z_back, x_back, y_fwd, t_back, yb_high, yb_low, xs, h_rows, mixed_s, mix_kron, acc,
    send1, send2, send3, send4, recv1, recv2, recv3, recv4, ring_s, ring_r, plane_s, plane_r,
    in_sem, w_sem, out_sem, sg_sem, send_sem, recv_sem, small_send, small_recv,
):
    gz, ta = lax.axis_index("gz"), lax.axis_index("ta")
    core = lax.rem(gz, 2)
    z = lax.rem(gz // 2, 8)
    x = ta * 2 + lax.rem(gz // 16, 2)
    y = gz // 32
    me = gz * 2 + ta

    def load(k, src, dst):
        return pltpu.make_async_copy(src, dst, in_sem.at[k])

    field_in = [load(t, field_h.at[pl.ds(t * C, C)], field.at[pl.ds(t * C, C)]) for t in range(TD)]
    rest_in = [
        load(5, cot_h, cot), load(6, t_back_h, t_back), load(7, yb_high_h, yb_high), load(8, yb_low_h, yb_low),
        load(10, mix_h, mix), load(11, z_fwd_h, z_fwd), load(12, z_back_h, z_back), load(13, x_back_h, x_back),
    ]
    table_in = [load(4, y_fwd_h, y_fwd), load(9, x_fwd_h, x_fwd)]
    w_in = [pltpu.make_async_copy(weight_h, w_raw, w_sem.at[0])]
    barrier = pltpu.get_barrier_semaphore()

    steps = sorted(((dy, dx) for dy in range(4) for dx in range(4)), key=lambda d: -(min(d[0], 4 - d[0]) + min(d[1], 4 - d[1])))
    ys, xs_ = [lax.rem(y + d, 4) for d in range(4)], [lax.rem(x + d, 4) for d in range(4)]
    plane = [(ys[dy] * 2 + lax.rem(xs_[dx], 2), xs_[dx] // 2) for dy, dx in steps]

    def each_peer(do):
        def step(kz, _):
            pz = lax.rem(z + 4 + ((kz + 1) // 2) * (1 - 2 * lax.rem(kz, 2)), 8)
            for p, t in plane:
                do(p, pz, core, t)
                do(p, pz, 1 - core, t)
            return 0

        lax.fori_loop(0, 7, step, 0)
        for p, t in plane[:-1]:
            do(p, z, core, t)
            do(p, z, 1 - core, t)
        do(*plane[-1][:1], z, 1 - core, ta)

    def greet(p, pz, c, t):
        pl.semaphore_signal(barrier, inc=1, device_id=(p * 16 + pz * 2 + c, t), device_id_type=MESH)

    def exchange(k, source, target):
        pltpu.make_async_copy(source(gz // 16, z, core, ta), target, recv_sem.at[k]).start()

        def send(p, pz, c, t):
            pltpu.make_async_remote_copy(
                src_ref=source(p, pz, c, t), dst_ref=target, send_sem=send_sem.at[k], recv_sem=recv_sem.at[k],
                device_id=(p * 16 + pz * 2 + c, t), device_id_type=MESH,
            ).start()

        each_peer(send)

    def arrived(k, whole):
        pltpu.make_async_copy(whole, whole, recv_sem.at[k]).wait()

    def by_mode(buffer):
        return lambda p, pz, c, t: buffer.at[p * 2 + pz // 4, lax.rem(pz, 4) * 4 + c * 2 + t]

    def by_cell(buffer):
        return lambda p, pz, c, t: buffer.at[p * 16 + pz * 2 + c, t]

    def plane_modes(t, source):
        halves = [[source[t * C + half * CH + i] for i in range(CH)] for half in range(2)]
        y_done = dot(jnp.concatenate([jnp.concatenate(h, axis=1) for h in halves], axis=0), y_fwd[...])
        for half in range(2):
            high, low = split(y_done[half * NX : half * NX + NX])
            both = dot(x_fwd[...], jnp.concatenate([high, low], axis=0))
            xs[t * 2 + half] = both[:16] + both[16:]

    def mode_messages(send):
        parts = [xs[k] for k in range(GROUPS)]
        for h in range(2):
            mixed = []
            for f in range(TD):
                c = [t_fwd[h * TD + f, ta * TD + t] for t in range(TD)]
                for half in range(2):
                    mixed.append(sum(c[t] * parts[t * 2 + half] for t in range(TD)))
            for r in range(8):
                for j in range(2):
                    send[:, r * 2 + h, j, :] = jnp.concatenate(
                        [mixed[4 * j + i][:, r * 32 : r * 32 + 32] for i in range(4)], axis=1
                    )

    def spectrum(recv):
        flat = [jnp.transpose(dot(z_fwd[...], recv[:, j, :], HIGHEST)) for j in range(2)]
        blocks = []
        for b in range(2):
            for f in range(TD):
                rows = [((f % 2) * 4 + half * 2 + b) * 16 for half in range(2)]
                blocks.append(jnp.concatenate([flat[f // 2][r : r + 16] for r in rows], axis=0))
        return jnp.concatenate(blocks, axis=1)

    def cell_messages(modes, send):
        steps = jnp.transpose(dot(modes, t_back[ta], HIGHEST))
        pieces = []
        for t in range(NT):
            for half in range(2):
                for b in range(2):
                    row = (t * 2 + b) * 16
                    pieces.append(steps[row : row + 16, half * CP : half * CP + CP])
        high, low = split(jnp.concatenate(pieces, axis=1))
        cells = dot(z_back[...], jnp.concatenate([high, low, high], axis=0))
        for k in range(4):
            send[:, k // 2, k % 2, :] = cells[:, k * 128 : k * 128 + 128]

    def cell_rows(recv, out):
        rows = [[recv[:, 2 * r, j, :] + recv[:, 2 * r + 1, j, :] for j in range(2)] for r in range(8)]
        groups = []
        for k in range(GROUPS):
            at = (k % 4) * 32
            groups.append(jnp.concatenate([rows[r][k // 4][:, at : at + 32] for r in range(8)], axis=1))
        high, low = split(jnp.concatenate(groups, axis=0))
        both = jnp.concatenate([high, low], axis=0)
        for n in range(5):
            cut = slice(n * 256, n * 256 + 256)
            wide = dot(both, yb_high[:, cut])
            values = wide[:128] + wide[128:] + dot(high, yb_low[:, cut])
            top, rest = split(values)
            for k in range(GROUPS):
                out[k, 0:16, cut] = top[k * 16 : k * 16 + 16]
                out[k, 16:32, cut] = rest[k * 16 : k * 16 + 16]
                if out.shape[1] == 48:
                    out[k, 32:48, cut] = top[k * 16 : k * 16 + 16]

    def tile_rows(source, t, xt):
        at = pl.multiple_of(xt * 16, 16)
        return source[pl.ds(t * C, C), pl.ds(at, 16), :].reshape(C * 16, NY)

    def pair_rows(source, pair, xt):
        return jnp.concatenate([tile_rows(source, pair * 2, xt), tile_rows(source, pair * 2 + 1, xt)], axis=1)

    def make_kron(transposed):
        pick = (lax.broadcasted_iota(jnp.int32, (C * 16, C), 0) // 16 == lax.broadcasted_iota(jnp.int32, (C * 16, C), 1)).astype(BF16)
        dims = (((1,), (1 if transposed else 0,)), ((), ()))
        tall = lax.dot_general(pick, mix[...], dims, preferred_element_type=F32).astype(BF16)
        wide = lax.dot_general(tall, pick, (((1,), (1,)), ((), ())), preferred_element_type=F32)
        same = lax.rem(lax.broadcasted_iota(jnp.int32, wide.shape, 0), 16) == lax.rem(lax.broadcasted_iota(jnp.int32, wide.shape, 1), 16)
        mix_kron[...] = jnp.where(same, wide, 0.0).astype(BF16)

    def channel_mix(source, pair, add_bias):
        def step(xt, _):
            out = dot(mix_kron[...], pair_rows(source, pair, xt))
            at = pl.multiple_of(xt * 16, 16)
            for i in range(2):
                for o in range(C):
                    part = out[o * 16 : o * 16 + 16, i * 128 : i * 128 + 128]
                    lin[(pair * 2 + i) * C + o, pl.ds(at, 16), :] = part + bias[o] if add_bias else part
            return 0

        lax.fori_loop(0, 8, step, 0)

    each_peer(greet)
    for copy in table_in + field_in + w_in + rest_in:
        copy.start()
    for copy in table_in + field_in:
        copy.wait()

    def field_step(k, _):
        plane_modes(k, field)
        return 0

    lax.fori_loop(0, TD, field_step, 0)
    mode_messages(send1)
    pl.semaphore_wait(barrier, 255)
    exchange(0, by_mode(send1), recv1.at[me])
    for copy in rest_in + w_in:
        copy.wait()
    make_kron(False)
    for pair in range(2):
        channel_mix(field, pair, True)
    w_t[...] = jnp.zeros_like(w_t)
    for o in range(C):
        turned = jnp.transpose(jnp.concatenate([w_raw[:, o, b, :] for b in range(2)], axis=0))
        w_t[o, 0:CH, :] = turned[:CH]
        w_t[o, CP : CP + CH, :] = turned[CH:]
    mixed_s[...] = jnp.zeros_like(mixed_s)
    arrived(0, recv1)
    field_spec = spectrum(recv1)
    for o in range(C):
        row = o if o < CH else o - CH + CP
        mixed_s[row : row + 1, :] = jnp.sum(w_t[o] * field_spec, axis=0, keepdims=True)
    cell_messages(mixed_s[...], send2)
    exchange(1, by_cell(send2), recv2.at[gz // 8, lax.rem(gz, 8) * 2 + ta])
    make_kron(True)
    acc[...] = jnp.zeros_like(acc)
    arrived(1, recv2)
    cell_rows(recv2, h_rows)

    def grad_step(t, _):
        for half in range(2):
            for n in range(5):
                pair = dot(x_back[...], h_rows[t * 2 + half, :, n * 256 : n * 256 + 256])
                for i in range(2):
                    p = t * C + half * CH + n * 2 + i
                    slope = gelu_slope(lin[p] + pair[:, i * 128 : i * 128 + 128])
                    grad[p] = (cot[p].astype(F32) * slope).astype(BF16)
        plane_modes(t, grad)
        return 0

    lax.fori_loop(0, TD, grad_step, 0, unroll=2)
    mode_messages(send3)
    exchange(2, by_mode(send3), recv3.at[me])

    def sum_step(k, _):
        pair, xt = lax.rem(k, 2), k // 2
        left = jnp.concatenate([pair_rows(field, pair, xt), jnp.ones((16, 256), BF16)], axis=0)
        acc[...] += lax.dot_general(
            left, pair_rows(grad, pair, xt), (((1,), (1,)), ((), ())), preferred_element_type=F32
        )
        return 0

    lax.fori_loop(0, 16, sum_step, 0)
    shape = acc.shape
    same = lax.rem(lax.broadcasted_iota(jnp.int32, shape, 0), 16) == lax.rem(lax.broadcasted_iota(jnp.int32, shape, 1), 16)
    kept = jnp.where(same, acc[...], 0.0)
    rows = (lax.broadcasted_iota(jnp.int32, (24, shape[0]), 1) // 16 == lax.broadcasted_iota(jnp.int32, (24, shape[0]), 0)).astype(F32)
    lanes = (lax.broadcasted_iota(jnp.int32, (shape[1], 32), 0) // 16 == lax.broadcasted_iota(jnp.int32, (shape[1], 32), 1)).astype(F32)
    sums = dot(dot(rows, kept, HIGHEST), lanes, HIGHEST)
    ring_s[...] = jnp.concatenate([sums[0:8], sums[8:16], sums[16:24], jnp.zeros((8, 32), F32)], axis=1)
    p, q = gz // 16, lax.rem(gz, 16)

    def small(k, source, target, peer):
        return pltpu.make_async_remote_copy(
            src_ref=source, dst_ref=target, send_sem=small_send.at[k], recv_sem=small_recv.at[k],
            device_id=peer, device_id_type=MESH,
        )

    pltpu.make_async_copy(ring_s, ring_r.at[q], small_recv.at[0]).start()

    def ring_step(d, _):
        small(0, ring_s, ring_r.at[q], (p * 16 + lax.rem(q + d, 16), ta)).start()
        return 0

    lax.fori_loop(1, 16, ring_step, 0)
    arrived(2, recv3)
    grad_spec = spectrum(recv3)
    back = jnp.zeros((32, 128), F32)
    for o in range(C):
        row = o if o < CH else o - CH + CP
        back = back + w_t[o] * grad_spec[row : row + 1]
    cell_messages(back, send4)
    exchange(3, by_cell(send4), recv4.at[gz // 8, lax.rem(gz, 8) * 2 + ta])
    pltpu.make_async_copy(ring_r, ring_r, small_recv.at[0]).wait()
    total = ring_r[0]
    for i in range(1, 16):
        total = total + ring_r[i]
    plane_s[...] = total
    v = p * 2 + ta
    pltpu.make_async_copy(plane_s, plane_r.at[v], small_recv.at[1]).start()

    def plane_step(d, _):
        u = lax.rem(v + d, 16)
        small(1, plane_s, plane_r.at[v], ((u // 2) * 16 + q, lax.rem(u, 2))).start()
        return 0

    lax.fori_loop(1, 16, plane_step, 0)
    half_planes = [pl.ds(pair * 2 * C, 2 * C) for pair in range(2)]
    lin_out = [pltpu.make_async_copy(lin.at[at], lin_o.at[at], out_sem.at[pair]) for pair, at in enumerate(half_planes)]
    for pair in range(2):
        channel_mix(grad, pair, False)
        lin_out[pair].start()
    for o in range(C):
        row = o if o < CH else o - CH + CP
        turned = jnp.transpose(field_spec * grad_spec[row : row + 1])
        for b in range(2):
            part = turned[b * 64 : b * 64 + 64]
            sg_raw[:, o, b, :] = jnp.concatenate([part[:, :CH], part[:, CP : CP + CH]], axis=1)
    sg_out = [pltpu.make_async_copy(sg_raw, sg_o, sg_sem.at[0])]
    for copy in sg_out:
        copy.start()
    arrived(3, recv4)
    cell_rows(recv4, cells_o)
    pltpu.make_async_copy(plane_r, plane_r, small_recv.at[1]).wait()
    total = plane_r[0]
    for i in range(1, 16):
        total = total + plane_r[i]
    sums_o[...] = total
    for copy in sg_out + lin_out:
        copy.wait()
    for k in range(4):
        sent = recv1.at[pl.ds(0, 255)]
        pltpu.make_async_copy(sent, sent, send_sem.at[k]).wait()
    for k in range(2):
        sent = ring_r.at[pl.ds(0, 15)]
        pltpu.make_async_copy(sent, sent, small_send.at[k]).wait()


def last_kernel(
    lin_h, cells_h, x_back_h, sums_h, sg_h, out_h, wg_h, bg_h, sg_out_h,
    lin, cells, x_back, sums, staged, out, wg, bg, lin_sem, cells_sem, out_sem, sem,
):
    def part(k, n=1):
        return pl.ds(k * n, n)

    x_in = pltpu.make_async_copy(x_back_h, x_back, sem.at[0])
    sums_in = pltpu.make_async_copy(sums_h, sums, sem.at[1])
    sg_in = pltpu.make_async_copy(sg_h, staged, sem.at[2])
    sg_out = pltpu.make_async_copy(staged, sg_out_h, sem.at[3])
    wg_out = pltpu.make_async_copy(wg, wg_h, sem.at[4])
    bg_out = pltpu.make_async_copy(bg, bg_h, sem.at[5])
    cells_in = [pltpu.make_async_copy(cells_h.at[part(k)], cells.at[part(k)], cells_sem.at[k]) for k in range(GROUPS)]
    lin_in = [pltpu.make_async_copy(lin_h.at[part(k, CH)], lin.at[part(k, CH)], lin_sem.at[k]) for k in range(GROUPS)]
    field_out = [pltpu.make_async_copy(out.at[part(k, CH)], out_h.at[part(k, CH)], out_sem.at[k]) for k in range(GROUPS)]
    x_in.start()
    for k in range(GROUPS):
        cells_in[k].start()
        lin_in[k].start()
        if k == 1:
            sums_in.start()
            sg_in.start()
    x_in.wait()
    for k in range(GROUPS):
        cells_in[k].wait()
        lin_in[k].wait()
        for n in range(5):
            part_k = cells[k, :, n * 256 : n * 256 + 256]
            pair = dot(x_back[...], jnp.concatenate([part_k, part_k[:16]], axis=0))
            for i in range(2):
                p = k * CH + n * 2 + i
                out[p] = (lin[p] + pair[:, i * 128 : i * 128 + 128]).astype(BF16)
        field_out[k].start()
        if k == 3:
            sums_in.wait()
            scale = 1.0 / math.sqrt(NX * NY * NZ * NT)
            rows = jnp.concatenate([sums[:, 32 * i : 32 * i + 32] for i in range(3)], axis=0) * scale
            wg[...] = jnp.transpose(rows)[:C, :C]
            bg[...] = rows[C : C + 1, :C]
            wg_out.start()
            bg_out.start()
            sg_in.wait()
            sg_out.start()
    for copy in [*field_out, wg_out, bg_out, sg_out]:
        copy.wait()


def per_device(field, cotangent, mix_weight, bias, spectral_weight):
    tab = tables()
    shape = field.shape
    planes = (PLANES, NX, NY)
    weight = jnp.transpose(spectral_weight, (0, 1, 3, 2, 4)).reshape(64, C, 2, C)
    modes = (64, C, 2, C)
    any_, hbm, vmem, smem = (pl.BlockSpec(memory_space=m) for m in (pl.ANY, pltpu.HBM, pltpu.VMEM, pltpu.SMEM))
    dma = pltpu.SemaphoreType.DMA
    sent, cells = pltpu.VMEM((16, 16, 2, 128), F32), pltpu.VMEM((128, 2, 2, 128), F32)
    rows = pltpu.VMEM((256, 2, 128), F32)
    small = pltpu.VMEM((16, 8, 128), F32)
    lin, sg, h_rows, sums = pl.pallas_call(
        main_kernel,
        out_shape=(
            jax.ShapeDtypeStruct(planes, F32),
            jax.ShapeDtypeStruct(modes, F32),
            jax.ShapeDtypeStruct((GROUPS, 32, CH * NY), BF16),
            jax.ShapeDtypeStruct((8, 128), F32),
        ),
        in_specs=[hbm] * 4 + [smem] * 2 + [hbm] * 8,
        out_specs=(any_, any_, vmem, vmem),
        scratch_shapes=[
            pltpu.VMEM(planes, BF16), pltpu.VMEM(planes, BF16), pltpu.VMEM(planes, BF16), pltpu.VMEM(planes, F32),
            pltpu.VMEM(modes, F32), pltpu.VMEM((C, 32, 128), F32), pltpu.VMEM(modes, F32),
            pltpu.VMEM((C, C), BF16), pltpu.VMEM((32, 256), BF16), pltpu.VMEM((16, 256), F32),
            pltpu.VMEM((128, 48), BF16), pltpu.VMEM((128, 48), BF16),
            pltpu.VMEM((CH * NY, 256), BF16), pltpu.VMEM((2, 128, 256), F32),
            pltpu.VMEM((256, CH * NY), BF16), pltpu.VMEM((256, CH * NY), BF16),
            pltpu.VMEM((GROUPS, 16, 256), F32), pltpu.VMEM((GROUPS, 48, CH * NY), BF16), pltpu.VMEM((32, 128), F32),
            pltpu.VMEM((C * 16, C * 16), BF16), pltpu.VMEM((C * 16 + 16, C * 16), F32),
            sent, cells, sent, cells, rows, sent, rows, sent,
            pltpu.VMEM((8, 128), F32), small, pltpu.VMEM((8, 128), F32), small,
            dma((14,)), dma((1,)), dma((2,)), dma((1,)), dma((4,)), dma((4,)), dma((2,)), dma((2,)),
        ],
        compiler_params=pltpu.CompilerParams(collective_id=0, has_side_effects=True, vmem_limit_bytes=57 * 2**20),
    )(
        field.reshape(planes), cotangent.reshape(planes), weight, mix_weight, bias,
        tab["t_fwd"], tab["x_fwd"], tab["z_fwd"], tab["z_back"], tab["x_back"],
        tab["y_fwd"], tab["t_back"], tab["yb_high"], tab["yb_low"],
    )
    field_grad, wg, bg, sg = pl.pallas_call(
        last_kernel,
        out_shape=(
            jax.ShapeDtypeStruct(planes, BF16),
            jax.ShapeDtypeStruct((C, C), F32),
            jax.ShapeDtypeStruct((1, C), F32),
            jax.ShapeDtypeStruct(modes, F32),
        ),
        in_specs=[any_] * 5,
        out_specs=(any_,) * 4,
        scratch_shapes=[
            pltpu.VMEM(planes, F32), pltpu.VMEM((GROUPS, 32, CH * NY), BF16), pltpu.VMEM((NX, 48), BF16),
            pltpu.VMEM((8, 128), F32), pltpu.VMEM(modes, F32), pltpu.VMEM(planes, BF16),
            pltpu.VMEM((C, C), F32), pltpu.VMEM((1, C), F32),
            dma((GROUPS,)), dma((GROUPS,)), dma((GROUPS,)), dma((6,)),
        ],
        compiler_params=pltpu.CompilerParams(vmem_limit_bytes=60 * 2**20),
    )(lin, h_rows, tab["x_back"], sums, sg)
    sg = jnp.transpose(sg.reshape(TD, 16, C, 2, C), (0, 1, 3, 2, 4))
    return field_grad.reshape(shape), wg, bg.reshape(C), sg


def solution(mesh):
    return jax.shard_map(
        per_device,
        mesh=mesh,
        in_specs=(
            P("ta", "gz", None, None, None),
            P("ta", "gz", None, None, None),
            P(),
            P(),
            P("ta", None, "gz", None, None),
        ),
        out_specs=(P("ta", "gz", None, None, None), P(), P(), P("ta", None, "gz", None, None)),
        check_vma=False,
    )
```
